32 devices in a mesh: ta: 8 (over y, x, core), gz: 4 (over z).
Axes of the slice: x: 2, y: 2, z: 4, core: 2. Of those that a mesh axis runs over, the one named last changes fastest.
Arguments:
- links: float32 [4, 18, 4, 64, 256], P(None, None, 'gz', 'ta'), may hold values from -1 to 1, as said below
- source: float32 [24, 4, 64, 256], P(None, 'gz', 'ta'), may hold values from -6 to 6
Outputs:
- solution: float32 [24, 4, 64, 256], P(None, 'gz', 'ta')
- residual: float32 [24, 4, 64, 256], P(None, 'gz', 'ta')
The draws below stay inside these ranges and needn't reach their ends.
Inputs may be any that keep to these rules, and one draw needn't show every extreme that they name: `links`: every link is a unitary 3x3 complex matrix.
All inputs are finite; a program needn't handle non-finite values.
Results may differ from the reference program's by a relative error of at most 0.00027.
Values sent between devices are 32-bit elements; how exact they have to be, the bound alone decides.
A program may use at most 256 MiB of HBM per device.

```python
import jax
import jax.numpy as jnp
from jax import lax

LX = 16
LY = 16
CT = 8
CZ = 1
NMR = 4
NZ = 4
NT = 64
N_TA = 8
N_GZ = 4


def draw_links(key, part):
    plane_sites = LX * LY
    noise = jax.random.normal(key, (2, 3, 3, 4, NZ, NT, plane_sites), jnp.float32)
    matrix_real = noise[0]
    matrix_imag = noise[1]
    rows_real = []
    rows_imag = []
    for row_index in range(3):
        vector_real = matrix_real[row_index]
        vector_imag = matrix_imag[row_index]
        for earlier in range(row_index):
            prior_real = rows_real[earlier]
            prior_imag = rows_imag[earlier]
            project_real = jnp.sum(prior_real * vector_real + prior_imag * vector_imag, axis=0)
            project_imag = jnp.sum(prior_real * vector_imag - prior_imag * vector_real, axis=0)
            vector_real = vector_real - (project_real * prior_real - project_imag * prior_imag)
            vector_imag = vector_imag - (project_real * prior_imag + project_imag * prior_real)
        squared_length = jnp.sum(vector_real * vector_real + vector_imag * vector_imag, axis=0)
        inverse_length = lax.rsqrt(jnp.maximum(squared_length, 1e-12))
        rows_real.append(vector_real * inverse_length)
        rows_imag.append(vector_imag * inverse_length)
    unitary = jnp.stack([jnp.stack(rows_real), jnp.stack(rows_imag)])
    return jnp.transpose(unitary, (3, 0, 1, 2, 4, 5, 6)).reshape((4, 18, NZ, NT, plane_sites))


def level_of(key, dims, split, smallest, top_value):
    loudness = 1.0
    for dim, parts in split:
        heights = jax.random.uniform(jax.random.fold_in(jax.random.fold_in(key, 6), dim), (parts,), jnp.float32, smallest / len(split), top_value / len(split))
        loudness = loudness * jnp.repeat(jnp.exp(heights), dims[dim] // parts).reshape((-1,) + (1,) * (len(dims) - 1 - dim))
    return loudness


def normal_values(key, extent, width, most, split=(), kind=jnp.bfloat16):
    values = jax.random.normal(key, extent, jnp.float32) * width
    if len(split) > 0:
        values = level_of(key, extent, split, -0.22, 0.18) * values
    return jnp.clip(values, min=-most, max=most).astype(kind)


def setup_inputs(seed: int = 0) -> dict:
    key_of = jax.random.split(jax.random.key(seed), 3)
    links = draw_links(jax.random.fold_in(key_of[2], 71), 0)
    source = normal_values(key_of[1], (24, NZ, NT, LY * LX), 1.0, 6.0, ((1, 4), (2, 8)), jnp.float32)
    return {"links": links, "source": source}


bare_mass = 0.2
mean_epsilon = 1e-6
gamma_column = ((3, 2, 1, 0), (3, 2, 1, 0), (2, 3, 0, 1), (2, 3, 0, 1))
gamma_real = ((0, 0, 0, 0), (-1, 1, 1, -1), (0, 0, 0, 0), (1, 1, 1, 1))
gamma_imag = ((1, 1, -1, -1), (0, 0, 0, 0), (1, -1, -1, 1), (0, 0, 0, 0))


def spin_project(field, direction, orientation):
    trailing = field.shape[1:]
    spin_real = field[:12].reshape((4, 3) + trailing)
    spin_imag = field[12:].reshape((4, 3) + trailing)
    rows_real = []
    rows_imag = []
    for spin_row in range(4):
        source_row = gamma_column[direction][spin_row]
        coef_real = orientation * gamma_real[direction][spin_row]
        coef_imag = orientation * gamma_imag[direction][spin_row]
        if coef_real != 0:
            rows_real.append(spin_real[spin_row] + coef_real * spin_real[source_row])
            rows_imag.append(spin_imag[spin_row] + coef_real * spin_imag[source_row])
        else:
            rows_real.append(spin_real[spin_row] - coef_imag * spin_imag[source_row])
            rows_imag.append(spin_imag[spin_row] + coef_imag * spin_real[source_row])
    return jnp.concatenate([jnp.stack(rows_real).reshape((12,) + trailing), jnp.stack(rows_imag).reshape((12,) + trailing)], 0)


def color_apply(link, field, adjoint):
    trailing = field.shape[1:]
    link_real = link[:9].reshape((3, 3) + trailing)
    link_imag = link[9:].reshape((3, 3) + trailing)
    spin_real = field[:12].reshape((4, 3) + trailing)
    spin_imag = field[12:].reshape((4, 3) + trailing)
    out_real = []
    out_imag = []
    for out_color in range(3):
        total_real = None
        total_imag = None
        for in_color in range(3):
            if adjoint:
                entry_real = link_real[in_color, out_color]
                entry_imag = -link_imag[in_color, out_color]
            else:
                entry_real = link_real[out_color, in_color]
                entry_imag = link_imag[out_color, in_color]
            piece_real = entry_real * spin_real[:, in_color] - entry_imag * spin_imag[:, in_color]
            piece_imag = entry_real * spin_imag[:, in_color] + entry_imag * spin_real[:, in_color]
            total_real = piece_real if total_real is None else total_real + piece_real
            total_imag = piece_imag if total_imag is None else total_imag + piece_imag
        out_real.append(total_real)
        out_imag.append(total_imag)
    return jnp.concatenate([jnp.stack(out_real, 1).reshape((12,) + trailing), jnp.stack(out_imag, 1).reshape((12,) + trailing)], 0)


def dirac_terms(field, forward, backward, back_links, links):
    hopping = None
    for direction in range(4):
        contribution = spin_project(color_apply(links[direction], forward[direction], False), direction, -1.0)
        contribution = contribution + spin_project(color_apply(back_links[direction], backward[direction], True), direction, 1.0)
        hopping = contribution if hopping is None else hopping + contribution
    return (4.0 + bare_mass) * field - 0.5 * hopping


def displaced(field, direction, stride):
    if direction < 2:
        lattice_view = field.reshape(field.shape[:3] + (LY, LX))
        which_axis = 4 if direction == 0 else 3
        return jnp.roll(lattice_view, -stride, axis=which_axis).reshape(field.shape)
    return jnp.roll(field, -stride, axis=1 if direction == 2 else 2)


def full_operator(field, links):
    forward = [displaced(field, direction, 1) for direction in range(4)]
    backward = [displaced(field, direction, -1) for direction in range(4)]
    back_links = [displaced(links[direction], direction, -1) for direction in range(4)]
    return dirac_terms(field, forward, backward, back_links, links)


def edge_masks():
    plane = jnp.arange(LY * LX)
    coords = [plane % LX, plane // LX, jnp.arange(NZ), jnp.arange(NT)]
    extents = [LX // 2, LY // 2, CZ, CT]
    shapes = [(1, 1, 1, LY * LX), (1, 1, 1, LY * LX), (1, NZ, 1, 1), (1, 1, NT, 1)]
    ahead = []
    behind = []
    for direction in range(4):
        inner = coords[direction] % extents[direction]
        ahead.append((inner != extents[direction] - 1).astype(jnp.float32).reshape(shapes[direction]))
        behind.append((inner != 0).astype(jnp.float32).reshape(shapes[direction]))
    return ahead, behind


def block_operator(field, links, ahead, behind):
    forward = [displaced(field, direction, 1) * ahead[direction] for direction in range(4)]
    backward = [displaced(field, direction, -1) * behind[direction] for direction in range(4)]
    back_links = [displaced(links[direction], direction, -1) for direction in range(4)]
    return dirac_terms(field, forward, backward, back_links, links)


def block_sum(values):
    shaped = values.reshape((values.shape[0], N_GZ, CZ, N_TA, CT, 2, LY // 2, 2, LX // 2))
    return jnp.sum(shaped, axis=(0, 2, 4, 6, 8))


def spread(per_block):
    wide = jnp.broadcast_to(per_block[None, :, None, :, None, :, None, :, None], (1, N_GZ, CZ, N_TA, CT, 2, LY // 2, 2, LX // 2))
    return wide.reshape((1, NZ, NT, LY * LX))


def complex_scale(weight_real, weight_imag, field):
    scaled_real = weight_real * field[:12] - weight_imag * field[12:]
    scaled_imag = weight_real * field[12:] + weight_imag * field[:12]
    return jnp.concatenate([scaled_real, scaled_imag], 0)


def block_solve(residual, links, ahead, behind, active):
    remainder = residual * active
    update = jnp.zeros_like(residual)
    entries = 12 * (LX // 2) * (LY // 2) * CZ * CT
    for sweep in range(NMR):
        applied = block_operator(remainder, links, ahead, behind)
        margin_real = block_sum(applied[:12] * remainder[:12] + applied[12:] * remainder[12:]) / entries
        margin_imag = block_sum(applied[:12] * remainder[12:] - applied[12:] * remainder[:12]) / entries
        denominator = block_sum(applied * applied) / entries + mean_epsilon
        weight_real = spread(margin_real / denominator)
        weight_imag = spread(margin_imag / denominator)
        update = update + complex_scale(weight_real, weight_imag, remainder)
        remainder = remainder - complex_scale(weight_real, weight_imag, applied)
    return update


def schwarz_cycle(solution, source, links, ahead, behind):
    parity_table = (jnp.arange(N_GZ)[:, None, None, None] + jnp.arange(N_TA)[None, :, None, None] + jnp.arange(2)[None, None, :, None] + jnp.arange(2)[None, None, None, :]) % 2
    for colour in range(2):
        residual = source - full_operator(solution, links)
        active = spread((parity_table == colour).astype(jnp.float32))
        solution = solution + block_solve(residual, links, ahead, behind, active)
    return solution


def reference(links, source):
    ahead, behind = edge_masks()
    solution = schwarz_cycle(jnp.zeros_like(source), source, links, ahead, behind)
    half_block = CT // 2
    moved = schwarz_cycle(jnp.roll(solution, half_block, axis=2), jnp.roll(source, half_block, axis=2), jnp.roll(links, half_block, axis=3), ahead, behind)
    solution = jnp.roll(moved, -half_block, axis=2)
    residual = source - full_operator(solution, links)
    return solution, residual
```

```python
import jax
import jax.numpy as jnp
from jax import lax
from jax.experimental import pallas as pl
from jax.experimental.pallas import tpu as pltpu
from jax.sharding import PartitionSpec as P

LX = 16
LY = 16
NMR = 4
BX = LX // 2
BY = LY // 2
BARE = 4.0 + 0.2
EPSILON = 1e-06
COLUMN = ((3, 2, 1, 0), (3, 2, 1, 0), (2, 3, 0, 1), (2, 3, 0, 1))
GAMMA = ((1j, 1j, -1j, -1j), (-1, 1, 1, -1), (1j, -1j, -1j, 1j), (1, 1, 1, 1))
MESH = pl.DeviceIdType.MESH
FIELD = (24, 8, 128)


def iota(dim):
    return lax.broadcasted_iota(jnp.int32, (8, 128), dim)


def turn(value, shift, axis):
    return pltpu.roll(value, shift % value.shape[axis], axis)


def swap_halves(value):
    flat = value.reshape((-1, 8, 128))
    return turn(flat, 4, 1).reshape(value.shape)


def roll_sites(value, shift, axis):
    flat = value.reshape((-1, 8, 128))
    return turn(flat, shift, axis).reshape(value.shape)


def gather_lanes(value, index):
    return jnp.take_along_axis(value, index, axis=1)


def pack_kernel(links_ref, source_ref, links_out, source_out, upper_out):
    lane = iota(1)
    low = lane < 64
    cell = lane % 64 // BX * LX + lane % BX
    sub_low = iota(0) < 4
    first = cell + jnp.where(low, 0, BX)
    second = cell + jnp.where(low, BX, 0)

    def split(tile):
        a, b = tile[:, :128], tile[:, 128:]
        even = jnp.where(low, gather_lanes(a, first), gather_lanes(b, first))
        odd = jnp.where(low, gather_lanes(a, second), gather_lanes(b, second))
        return even, odd

    for k in range(24):
        even, odd = split(source_ref[k, 0])
        source_out[0, k] = even
        source_out[1, k] = odd
    for mu in range(4):
        for k in range(9):
            pair = []
            for part in range(2):
                halves = split(links_ref[mu, part * 9 + k, 0])
                halves = [-0.5 * half for half in halves]
                for kind in range(2):
                    links_out[kind, mu * 18 + part * 9 + k] = halves[kind]
                pair.append(halves)
            for kind in range(2):
                real, imag = pair[0][kind], pair[1][kind]
                upper_out[kind, mu * 9 + k] = jnp.where(sub_low, turn(real, 4, 0), imag)


def unpack_kernel(solution_ref, residual_ref, solution_out, residual_out):
    lane = iota(1)
    cell = lane // LX * BX + lane % BX
    left = lane % LX < BX
    for source, target in ((solution_ref, solution_out), (residual_ref, residual_out)):
        for k in range(24):
            even, odd = source[0, k], source[1, k]
            target[k, 0, :, :128] = jnp.where(left, gather_lanes(even, cell), gather_lanes(odd, cell))
            target[k, 0, :, 128:] = jnp.where(
                left, gather_lanes(odd, cell + 64), gather_lanes(even, cell + 64)
            )


def spins(field):
    return field[:12].reshape((4, 3, 8, 128)), field[12:].reshape((4, 3, 8, 128))


def phase(coef, real, imag):
    if coef == 1:
        return real, imag
    if coef == -1:
        return -real, -imag
    if coef == 1j:
        return -imag, real
    return imag, -real


def project(real, imag, mu, sign):
    rows_real, rows_imag = [], []
    for k in range(2):
        other = COLUMN[mu][k]
        add_real, add_imag = phase(sign * GAMMA[mu][k], real[other], imag[other])
        rows_real.append(real[k] + add_real)
        rows_imag.append(imag[k] + add_imag)
    return jnp.stack(rows_real), jnp.stack(rows_imag)


def matrix(link):
    return link[:9].reshape((3, 3, 8, 128)), link[9:].reshape((3, 3, 8, 128))


def times(link, half):
    (ur, ui), (hr, hi) = link, half
    out_real = out_imag = None
    for b in range(3):
        vr, vi = hr[:, b][:, None], hi[:, b][:, None]
        mr, mi = ur[:, b][None], ui[:, b][None]
        pr, pi = mr * vr - mi * vi, mr * vi + mi * vr
        out_real = pr if out_real is None else out_real + pr
        out_imag = pi if out_imag is None else out_imag + pi
    return out_real, out_imag


def adjoint_times(link, half):
    (ur, ui), (hr, hi) = link, half
    out_real = out_imag = None
    for b in range(3):
        vr, vi = hr[:, b][:, None], hi[:, b][:, None]
        mr, mi = ur[b][None], ui[b][None]
        pr, pi = mr * vr + mi * vi, mr * vi - mi * vr
        out_real = pr if out_real is None else out_real + pr
        out_imag = pi if out_imag is None else out_imag + pi
    return out_real, out_imag


def expand(total, half, mu, sign):
    hr, hi = half
    total_real, total_imag = list(total[0]), list(total[1])
    for k in range(4):
        if k < 2:
            add_real, add_imag = hr[k], hi[k]
        else:
            other = COLUMN[mu][k]
            add_real, add_imag = phase(sign * GAMMA[mu][k], hr[other], hi[other])
        total_real[k] = total_real[k] + add_real
        total_imag[k] = total_imag[k] + add_imag
    return total_real, total_imag


def moved(half, shift, axis):
    return roll_sites(half[0], shift, axis), roll_sites(half[1], shift, axis)


def masked(link, keep):
    return jnp.where(keep[None], link, 0.0)


INNER = {0: (2, -1, 7), 1: (2, -8, -8), 3: (1, -1, -1)}


def edges(time_edge):
    lane, time = iota(1), iota(0)
    return {
        0: lane % BX == BX - 1,
        1: lane // BX % BY == BY - 1,
        3: time == time_edge,
    }


def solve(links_of, rho, update, inner_links):
    edge = edges(7)
    for place, mu in enumerate((0, 1, 3)):
        inner_links[place] = masked(links_of(mu), jnp.logical_not(edge[mu]))
    update[...] = jnp.zeros(FIELD, jnp.float32)
    lane, time = iota(1), iota(0)
    low = lane < 64
    entries = 12.0 * 8 * BX * BY

    def step(_, carry):
        field = rho[...]
        real, imag = spins(field)
        total = (
            [BARE * real[k] for k in range(4)],
            [BARE * imag[k] for k in range(4)],
        )
        for place, mu in enumerate((0, 1, 3)):
            axis, shift, _ = INNER[mu]
            link = matrix(inner_links[place])
            ahead = moved(project(real, imag, mu, -1), shift, axis)
            total = expand(total, times(link, ahead), mu, -1)
            behind = adjoint_times(link, project(real, imag, mu, 1))
            total = expand(total, moved(behind, -shift, axis), mu, 1)
        ar = jnp.stack(total[0]).reshape((12, 8, 128))
        ai = jnp.stack(total[1]).reshape((12, 8, 128))
        fr, fi = field[:12], field[12:]
        sums = [
            jnp.sum(ar * fr + ai * fi, axis=0),
            jnp.sum(ar * fi - ai * fr, axis=0),
            jnp.sum(ar * ar + ai * ai, axis=0),
        ]
        rows = [jnp.sum(value, axis=0, keepdims=True) for value in sums]
        table = jnp.where(time == 0, rows[0], jnp.where(time == 1, rows[1], rows[2]))
        below = jnp.sum(jnp.where(low, table, 0.0), axis=1, keepdims=True)
        above = jnp.sum(jnp.where(low, 0.0, table), axis=1, keepdims=True)
        table = jnp.where(low, below, above) / entries
        scale = 1.0 / (table[2:3] + EPSILON)
        wr = jnp.broadcast_to(table[0:1] * scale, (8, 128))[None]
        wi = jnp.broadcast_to(table[1:2] * scale, (8, 128))[None]
        update[:12] = update[:12] + (wr * fr - wi * fi)
        update[12:] = update[12:] + (wr * fi + wi * fr)
        rho[:12] = fr - (wr * ar - wi * ai)
        rho[12:] = fi - (wr * ai + wi * ar)
        return carry

    lax.fori_loop(0, NMR, step, 0)


def nothing():
    zero = jnp.zeros((3, 8, 128), jnp.float32)
    return [zero] * 4, [zero] * 4


def cross_plane(total, real, imag, source_links, target_links, directions, edge):
    for mu in directions:
        axis, inner, shift = INNER[mu]
        ahead = moved(project(real, imag, mu, -1), shift, axis)
        link = matrix(masked(target_links(mu), edge[mu]))
        total = expand(total, times(link, ahead), mu, -1)
        link = matrix(masked(source_links(mu), edge[mu]))
        behind = adjoint_times(link, project(real, imag, mu, 1))
        total = expand(total, moved(behind, -shift, axis), mu, 1)
    return total


def joined(total):
    return (
        jnp.stack(total[0]).reshape((12, 8, 128)),
        jnp.stack(total[1]).reshape((12, 8, 128)),
    )


def flat(half):
    return half.reshape((6, 8, 128))


def upper_pack(real, imag, low):
    return jnp.where(low, swap_halves(real), imag)


def lower_pack(real, imag, low):
    return jnp.where(low, real, swap_halves(imag))


def forward_join(packed, own_real, own_imag, low):
    real = jnp.where(low, packed, swap_halves(own_real))
    imag = swap_halves(jnp.where(low, own_imag, packed))
    return real, imag


def back_join(packed, own_real, own_imag, low):
    real = swap_halves(jnp.where(low, packed, own_real))
    imag = jnp.where(low, swap_halves(own_imag), packed)
    return real, imag


def main_kernel(
    links, source, upper, solution_out, residual_out,
    moved_links, inner_links, rho, update, psi, res, back,
    links_in, halo_out, halo_in, time_out, time_in, last_out, last_in, send_sem, recv_sem,
):
    ta, gz = lax.axis_index("ta"), lax.axis_index("gz")
    n_ta, n_gz = lax.axis_size("ta"), lax.axis_size("gz")
    ta_next, ta_prev = lax.rem(ta + 1, n_ta), lax.rem(ta + n_ta - 1, n_ta)
    gz_next, gz_prev = lax.rem(gz + 1, n_gz), lax.rem(gz + n_gz - 1, n_gz)
    here = lax.rem(ta + gz, 2)
    kinds = (here, 1 - here)
    low = iota(0) < 4

    barrier = pltpu.get_barrier_semaphore()
    partners = [
        (ta_next, gz), (ta_prev, gz), (ta, gz_next), (ta, gz_prev),
        (ta_next, gz_next), (ta_next, gz_prev), (ta_prev, gz_next), (ta_prev, gz_prev),
    ]
    for partner in partners:
        pl.semaphore_signal(barrier, inc=1, device_id=partner, device_id_type=MESH)
    pl.semaphore_wait(barrier, len(partners))

    started = []

    def send(src, dst, device):
        place = len(started)
        copy = pltpu.make_async_remote_copy(
            src_ref=src, dst_ref=dst, send_sem=send_sem.at[place], recv_sem=recv_sem.at[place],
            device_id=device, device_id_type=MESH,
        )
        copy.start()
        started.append(copy)
        return copy

    link_copies = [send(upper.at[k], links_in.at[k], (ta_next, gz)) for k in range(2)]

    def first_links(kind):
        return lambda mu: links[kind, mu * 18 : mu * 18 + 18]

    def second_links(kind):
        return lambda mu: moved_links[kind, mu * 18 : mu * 18 + 18]

    def cross(number, origin, target, links_by_kind):
        real, imag = spins(update[...])
        from_links, to_links = links_by_kind(origin), links_by_kind(target)
        copies = []
        for place, mu in enumerate((2, 3)):
            lower_device = (ta, gz_prev) if mu == 2 else (ta_prev, gz)
            upper_device = (ta, gz_next) if mu == 2 else (ta_next, gz)
            ahead = project(real, imag, mu, -1)
            behind = adjoint_times(matrix(from_links(mu)), project(real, imag, mu, 1))
            for way, half, device in ((0, ahead, lower_device), (1, behind, upper_device)):
                slot = place * 2 + way
                halo_out[number, slot, :6] = flat(half[0])
                halo_out[number, slot, 6:] = flat(half[1])
                copies.append(
                    send(halo_out.at[number, slot], halo_in.at[number, slot], device)
                )
        total = cross_plane(nothing(), real, imag, from_links, to_links, (0, 1), edges(7))
        return total, copies, to_links

    def finish(number, total, copies, to_links):
        def landed(slot):
            copies[slot].wait_recv()
            value = halo_in[number, slot]
            return value[:6].reshape((2, 3, 8, 128)), value[6:].reshape((2, 3, 8, 128))

        time = iota(0)
        ahead = moved(landed(2), -1, 1)
        total = expand(total, times(matrix(masked(to_links(3), time == 7)), ahead), 3, -1)
        behind = landed(3)
        behind = [jnp.where(time == 0, roll_sites(value, 1, 1), 0.0) for value in behind]
        total = expand(total, behind, 3, 1)
        total = expand(total, times(matrix(to_links(2)), landed(0)), 2, -1)
        total = expand(total, landed(1), 2, 1)
        return joined(total)

    rho[...] = source[kinds[0]]
    solve(first_links(kinds[0]), rho, update, inner_links)
    psi[0] = update[...]
    res[0] = rho[...]
    pending = cross(0, kinds[0], kinds[1], first_links)
    hop = finish(0, *pending)
    rho[:12] = source[kinds[1], :12] - hop[0]
    rho[12:] = source[kinds[1], 12:] - hop[1]
    solve(first_links(kinds[1]), rho, update, inner_links)
    psi[1] = update[...]
    res[1] = rho[...]
    time_out[0] = upper_pack(rho[:12], rho[12:], low)
    pending = cross(1, kinds[1], kinds[0], first_links)
    turned = [send(time_out.at[0], time_in.at[0], (ta_next, gz))]
    for k in range(2):
        link_copies[k].wait_recv()
        for mu in range(4):
            own = links[k, mu * 18 : mu * 18 + 18]
            real, imag = forward_join(links_in[k, mu * 9 : mu * 9 + 9], own[:9], own[9:], low)
            moved_links[k, mu * 18 : mu * 18 + 9] = real
            moved_links[k, mu * 18 + 9 : mu * 18 + 18] = imag
    hop = finish(1, *pending)
    own_real, own_imag = res[0, :12] - hop[0], res[0, 12:] - hop[1]
    time_out[1] = upper_pack(own_real, own_imag, low)
    turned.append(send(time_out.at[1], time_in.at[1], (ta_next, gz)))

    turned[0].wait_recv()
    real, imag = forward_join(time_in[0], own_real, own_imag, low)
    rho[:12] = real
    rho[12:] = imag
    solve(second_links(kinds[0]), rho, update, inner_links)
    back[0] = update[...]
    back[1] = rho[...]
    pending = cross(2, kinds[0], kinds[1], second_links)
    returned = []
    for k in range(2):
        time_out[2 + k] = lower_pack(back[k, :12], back[k, 12:], low)
        returned.append(send(time_out.at[2 + k], time_in.at[2 + k], (ta_prev, gz)))
    turned[1].wait_recv()
    real, imag = forward_join(time_in[1], res[1, :12], res[1, 12:], low)
    hop = finish(2, *pending)
    rho[:12] = real - hop[0]
    rho[12:] = imag - hop[1]
    solve(second_links(kinds[1]), rho, update, inner_links)

    real, imag = spins(update[...])
    ahead = project(real, imag, 2, -1)
    behind = adjoint_times(matrix(second_links(kinds[1])(2)), project(real, imag, 2, 1))
    depth = []
    for way, half, column in ((0, ahead, gz_prev), (1, behind, gz_next)):
        half_real, half_imag = flat(half[0]), flat(half[1])
        last_out[way, 0] = upper_pack(half_real, half_imag, low)
        last_out[way, 1] = lower_pack(half_real, half_imag, low)
        depth.append(send(last_out.at[way, 0], last_in.at[way, 0], (ta, column)))
        depth.append(send(last_out.at[way, 1], last_in.at[way, 1], (ta_prev, column)))
    for k, value in enumerate((update, rho)):
        time_out[4 + k] = lower_pack(value[:12], value[12:], low)
        returned.append(send(time_out.at[4 + k], time_in.at[4 + k], (ta_prev, gz)))

    def restored(k, own):
        returned[k].wait_recv()
        return back_join(time_in[2 + k], own[:12], own[12:], low)

    step0 = restored(0, back[0])
    left0 = restored(1, back[1])
    step1 = restored(2, update[...])

    def to_links(mu):
        return jnp.where(low, first_links(kinds[0])(mu), first_links(kinds[1])(mu))

    def from_links(mu):
        return jnp.where(low, first_links(kinds[1])(mu), first_links(kinds[0])(mu))

    real, imag = [part.reshape((4, 3, 8, 128)) for part in step1]
    total = cross_plane(nothing(), real, imag, from_links, to_links, (0, 1, 3), edges(3))
    for way in range(2):
        for half in range(2):
            depth[way * 2 + half].wait_recv()
    for way in range(2):
        high, deep = last_in[way, 0], last_in[way, 1]
        half = (
            jnp.where(low, high, swap_halves(deep)).reshape((2, 3, 8, 128)),
            jnp.where(low, swap_halves(high), deep).reshape((2, 3, 8, 128)),
        )
        if way == 0:
            total = expand(total, times(matrix(to_links(2)), half), 2, -1)
        else:
            total = expand(total, half, 2, 1)
    hop = joined(total)
    left1 = restored(3, rho[...])
    for part in range(2):
        rows = slice(12 * part, 12 * part + 12)
        a, b = step0[part], step1[part]
        solution_out[kinds[0], rows] = psi[0, rows] + jnp.where(low, a, b)
        solution_out[kinds[1], rows] = psi[1, rows] + jnp.where(low, b, a)
        a, b = left0[part] - hop[part], left1[part]
        residual_out[kinds[0], rows] = jnp.where(low, a, b)
        residual_out[kinds[1], rows] = jnp.where(low, b, a)
    for copy in started:
        copy.wait_send()


def per_device(links, source):
    f32 = jnp.float32
    vmem = pl.BlockSpec(memory_space=pltpu.VMEM)
    packed = jax.ShapeDtypeStruct((2,) + FIELD, f32)
    local_links, local_source, upper = pl.pallas_call(
        pack_kernel,
        out_shape=(
            jax.ShapeDtypeStruct((2, 72, 8, 128), f32), packed,
            jax.ShapeDtypeStruct((2, 36, 8, 128), f32),
        ),
        in_specs=[vmem] * 2,
        out_specs=[vmem] * 3,
        compiler_params=pltpu.CompilerParams(vmem_limit_bytes=24 * 2**20),
    )(links, source)
    copies = 2 + 12 + 2 + 4 + 4
    half = (12, 8, 128)
    result = pl.pallas_call(
        main_kernel,
        out_shape=(packed, packed),
        in_specs=[vmem] * 3,
        out_specs=[vmem] * 2,
        scratch_shapes=[
            pltpu.VMEM((2, 72, 8, 128), f32),
            pltpu.VMEM((3, 18, 8, 128), f32),
            pltpu.VMEM(FIELD, f32),
            pltpu.VMEM(FIELD, f32),
            pltpu.VMEM((2,) + FIELD, f32),
            pltpu.VMEM((2,) + FIELD, f32),
            pltpu.VMEM((2,) + FIELD, f32),
            pltpu.VMEM((2, 36, 8, 128), f32),
            pltpu.VMEM((3, 4) + half, f32),
            pltpu.VMEM((3, 4) + half, f32),
            pltpu.VMEM((6,) + half, f32),
            pltpu.VMEM((6,) + half, f32),
            pltpu.VMEM((2, 2, 6, 8, 128), f32),
            pltpu.VMEM((2, 2, 6, 8, 128), f32),
            pltpu.SemaphoreType.DMA((copies,)),
            pltpu.SemaphoreType.DMA((copies,)),
        ],
        compiler_params=pltpu.CompilerParams(
            collective_id=0, has_side_effects=True, vmem_limit_bytes=32 * 2**20
        ),
    )(local_links, local_source, upper)
    out = jax.ShapeDtypeStruct(source.shape, f32)
    return pl.pallas_call(
        unpack_kernel,
        out_shape=(out, out),
        in_specs=[vmem] * 2,
        out_specs=[vmem] * 2,
        compiler_params=pltpu.CompilerParams(vmem_limit_bytes=24 * 2**20),
    )(*result)


def solution(mesh):
    in_specs = (P(None, None, "gz", "ta", None), P(None, "gz", "ta", None))
    out_specs = (P(None, "gz", "ta", None), P(None, "gz", "ta", None))
    return jax.shard_map(
        per_device, mesh=mesh, in_specs=in_specs, out_specs=out_specs, check_vma=False
    )
```

```python
import jax
import jax.numpy as jnp
from jax import lax
from jax.experimental import pallas as pl
from jax.experimental.pallas import tpu as pltpu
from jax.sharding import PartitionSpec as P

LX = 16
LY = 16
NMR = 4
BX = LX // 2
BY = LY // 2
BARE = 4.0 + 0.2
EPSILON = 1e-06
COLUMN = ((3, 2, 1, 0), (3, 2, 1, 0), (2, 3, 0, 1), (2, 3, 0, 1))
GAMMA = ((1j, 1j, -1j, -1j), (-1, 1, 1, -1), (1j, -1j, -1j, 1j), (1, 1, 1, 1))
MESH = pl.DeviceIdType.MESH
FIELD = (24, 8, 128)


def iota(dim):
    return lax.broadcasted_iota(jnp.int32, (8, 128), dim)


def turn(value, shift, axis):
    return pltpu.roll(value, shift % value.shape[axis], axis)


def swap_halves(value):
    flat = value.reshape((-1, 8, 128))
    return turn(flat, 4, 1).reshape(value.shape)


def roll_sites(value, shift, axis):
    flat = value.reshape((-1, 8, 128))
    return turn(flat, shift, axis).reshape(value.shape)


def gather_lanes(value, index):
    return jnp.take_along_axis(value, index, axis=1)


def pack_kernel(links_far, source_far, links_out, source_out, upper_out, links_ref, source_ref, sems):
    loads = [pltpu.make_async_copy(source_far, source_ref, sems.at[4])]
    for mu in range(4):
        loads.append(pltpu.make_async_copy(links_far.at[mu], links_ref.at[mu], sems.at[mu]))
    for load in loads:
        load.start()
    lane = iota(1)
    low = lane < 64
    cell = lane % 64 // BX * LX + lane % BX
    sub_low = iota(0) < 4
    first = cell + jnp.where(low, 0, BX)
    second = cell + jnp.where(low, BX, 0)

    def split(tile):
        a, b = tile[:, :128], tile[:, 128:]
        even = jnp.where(low, gather_lanes(a, first), gather_lanes(b, first))
        odd = jnp.where(low, gather_lanes(a, second), gather_lanes(b, second))
        return even, odd

    loads[0].wait()
    for k in range(24):
        even, odd = split(source_ref[k, 0])
        source_out[0, k] = even
        source_out[1, k] = odd
    for mu in range(4):
        loads[1 + mu].wait()
        for k in range(9):
            pair = []
            for part in range(2):
                halves = split(links_ref[mu, part * 9 + k, 0])
                halves = [-0.5 * half for half in halves]
                for kind in range(2):
                    links_out[kind, mu * 18 + part * 9 + k] = halves[kind]
                pair.append(halves)
            for kind in range(2):
                real, imag = pair[0][kind], pair[1][kind]
                upper_out[kind, mu * 9 + k] = jnp.where(sub_low, turn(real, 4, 0), imag)


def unpack_kernel(solution_ref, residual_ref, solution_far, residual_far, solution_out, residual_out, sems):
    lane = iota(1)
    cell = lane // LX * BX + lane % BX
    left = lane % LX < BX
    stores = []
    for source, target, far in (
        (solution_ref, solution_out, solution_far), (residual_ref, residual_out, residual_far)
    ):
        for k in range(24):
            even, odd = source[0, k], source[1, k]
            target[k, 0, :, :128] = jnp.where(left, gather_lanes(even, cell), gather_lanes(odd, cell))
            target[k, 0, :, 128:] = jnp.where(
                left, gather_lanes(odd, cell + 64), gather_lanes(even, cell + 64)
            )
            if k % 12 == 11:
                rows = pl.ds(k - 11, 12)
                copy = pltpu.make_async_copy(target.at[rows], far.at[rows], sems.at[len(stores)])
                copy.start()
                stores.append(copy)
    for copy in stores:
        copy.wait()


def spin_rows(ref):
    return lambda k: (ref[3 * k : 3 * k + 3], ref[12 + 3 * k : 15 + 3 * k])


def add_phase(real, imag, coef, more_real, more_imag):
    if coef == 1:
        return real + more_real, imag + more_imag
    if coef == -1:
        return real - more_real, imag - more_imag
    if coef == 1j:
        return real - more_imag, imag + more_real
    return real + more_imag, imag - more_real


def project(load, mu, sign):
    rows = [
        add_phase(*load(k), sign * GAMMA[mu][k], *load(COLUMN[mu][k])) for k in range(2)
    ]
    return jnp.stack([row[0] for row in rows]), jnp.stack([row[1] for row in rows])


def matrix(link):
    return link[:9].reshape((3, 3, 8, 128)), link[9:].reshape((3, 3, 8, 128))


def times(link, half):
    (ur, ui), (hr, hi) = link, half
    out_real = out_imag = None
    for b in range(3):
        vr, vi = hr[:, b][:, None], hi[:, b][:, None]
        mr, mi = ur[:, b][None], ui[:, b][None]
        pr, pi = mr * vr - mi * vi, mr * vi + mi * vr
        out_real = pr if out_real is None else out_real + pr
        out_imag = pi if out_imag is None else out_imag + pi
    return out_real, out_imag


def adjoint_times(link, half):
    (ur, ui), (hr, hi) = link, half
    out_real = out_imag = None
    for b in range(3):
        vr, vi = hr[:, b][:, None], hi[:, b][:, None]
        mr, mi = ur[b][None], ui[b][None]
        pr, pi = mr * vr + mi * vi, mr * vi - mi * vr
        out_real = pr if out_real is None else out_real + pr
        out_imag = pi if out_imag is None else out_imag + pi
    return out_real, out_imag


def expand(total, half, mu, sign):
    hr, hi = half
    total_real, total_imag = list(total[0]), list(total[1])
    for k in range(4):
        coef = 1 if k < 2 else sign * GAMMA[mu][k]
        other = k if k < 2 else COLUMN[mu][k]
        total_real[k], total_imag[k] = add_phase(
            total_real[k], total_imag[k], coef, hr[other], hi[other]
        )
    return total_real, total_imag


def moved(half, shift, axis):
    return roll_sites(half[0], shift, axis), roll_sites(half[1], shift, axis)


def masked(link, keep):
    return jnp.where(keep[None], link, 0.0)


INNER = {0: (2, -1, 7), 1: (2, -8, -8), 3: (1, -1, -1)}


def edges(time_edge):
    lane, time = iota(1), iota(0)
    return {
        0: lane % BX == BX - 1,
        1: lane // BX % BY == BY - 1,
        3: time == time_edge,
    }


def mask_links(links_of, inner_links):
    edge = edges(7)
    for place, mu in enumerate((0, 1, 3)):
        inner_links[place] = masked(links_of(mu), jnp.logical_not(edge[mu]))


def joined(total):
    return (
        jnp.stack(total[0]).reshape((12, 8, 128)),
        jnp.stack(total[1]).reshape((12, 8, 128)),
    )


def block_operator(ref, inner_links):
    load = spin_rows(ref)
    total = None
    for place, mu in enumerate((0, 1, 3)):
        axis, shift, _ = INNER[mu]
        ahead = moved(project(load, mu, -1), shift, axis)
        if total is None:
            start = [load(k) for k in range(4)]
            total = ([BARE * row[0] for row in start], [BARE * row[1] for row in start])
        total = expand(total, times(matrix(inner_links[place]), ahead), mu, -1)
        behind = adjoint_times(matrix(inner_links[place]), project(load, mu, 1))
        total = expand(total, moved(behind, -shift, axis), mu, 1)
    return joined(total)


def block_weights(rho, applied):
    time = iota(0)
    low = iota(1) < 64
    entries = 12.0 * 8 * BX * BY
    sums = [jnp.zeros((8, 128), jnp.float32)] * 3
    for k in range(12):
        fr, fi, ar, ai = rho[k], rho[12 + k], applied[k], applied[12 + k]
        sums[0] = sums[0] + (ar * fr + ai * fi)
        sums[1] = sums[1] + (ar * fi - ai * fr)
        sums[2] = sums[2] + (ar * ar + ai * ai)
    rows = [jnp.sum(value, axis=0, keepdims=True) for value in sums]
    table = jnp.where(time == 0, rows[0], jnp.where(time == 1, rows[1], rows[2]))
    below = jnp.sum(jnp.where(low, table, 0.0), axis=1, keepdims=True)
    above = jnp.sum(jnp.where(low, 0.0, table), axis=1, keepdims=True)
    table = jnp.where(low, below, above) / entries
    scale = 1.0 / (table[2:3] + EPSILON)
    wr = jnp.broadcast_to(table[0:1] * scale, (8, 128))
    wi = jnp.broadcast_to(table[1:2] * scale, (8, 128))
    return wr, wi


def scaled(wr, wi, ref, k):
    real, imag = ref[k], ref[12 + k]
    return wr * real - wi * imag, wr * imag + wi * real


def solve(rho, update, applied, inner_links):
    update[...] = jnp.zeros(FIELD, jnp.float32)
    first = block_operator(rho, inner_links)
    applied[:12] = first[0]
    applied[12:] = first[1]

    def advance(wr, wi):
        for k in range(12):
            add_real, add_imag = scaled(wr, wi, rho, k)
            update[k] = update[k] + add_real
            update[12 + k] = update[12 + k] + add_imag
            take_real, take_imag = scaled(wr, wi, applied, k)
            rho[k] = rho[k] - take_real
            rho[12 + k] = rho[12 + k] - take_imag

    def step(_, carry):
        wr, wi = block_weights(rho, applied)
        real, imag = block_operator(applied, inner_links)
        advance(wr, wi)
        applied[:12] = applied[:12] - (wr * real - wi * imag)
        applied[12:] = applied[12:] - (wr * imag + wi * real)
        return carry

    lax.fori_loop(0, NMR - 1, step, 0)
    advance(*block_weights(rho, applied))


def nothing():
    zero = jnp.zeros((3, 8, 128), jnp.float32)
    return [zero] * 4, [zero] * 4


def cross_plane(total, load, source_links, target_links, directions, edge):
    for mu in directions:
        axis, inner, shift = INNER[mu]
        ahead = moved(project(load, mu, -1), shift, axis)
        link = matrix(masked(target_links(mu), edge[mu]))
        total = expand(total, times(link, ahead), mu, -1)
        link = matrix(masked(source_links(mu), edge[mu]))
        behind = adjoint_times(link, project(load, mu, 1))
        total = expand(total, moved(behind, -shift, axis), mu, 1)
    return total


def flat(half):
    return half.reshape((6, 8, 128))


def upper_pack(real, imag, low):
    return jnp.where(low, swap_halves(real), imag)


def lower_pack(real, imag, low):
    return jnp.where(low, real, swap_halves(imag))


def forward_join(packed, own_real, own_imag, low):
    real = jnp.where(low, packed, swap_halves(own_real))
    imag = swap_halves(jnp.where(low, own_imag, packed))
    return real, imag


def back_join(packed, own_real, own_imag, low):
    real = swap_halves(jnp.where(low, packed, own_real))
    imag = jnp.where(low, swap_halves(own_imag), packed)
    return real, imag


def main_kernel(
    links, source, upper, solution_out, residual_out,
    moved_links, inner_links, rho, update, applied, psi, res, back,
    links_in, halo_out, halo_in, rim_out, rim_in, time_out, time_in, last_out, last_in, send_sem, recv_sem,
):
    ta, gz = lax.axis_index("ta"), lax.axis_index("gz")
    n_ta, n_gz = lax.axis_size("ta"), lax.axis_size("gz")
    ta_next, ta_prev = lax.rem(ta + 1, n_ta), lax.rem(ta + n_ta - 1, n_ta)
    gz_next, gz_prev = lax.rem(gz + 1, n_gz), lax.rem(gz + n_gz - 1, n_gz)
    here = lax.rem(ta + gz, 2)
    kinds = (here, 1 - here)
    low = iota(0) < 4

    barrier = pltpu.get_barrier_semaphore()
    partners = [
        (ta_next, gz), (ta_prev, gz), (ta, gz_next), (ta, gz_prev),
        (ta_next, gz_next), (ta_next, gz_prev), (ta_prev, gz_next), (ta_prev, gz_prev),
    ]
    for partner in partners:
        pl.semaphore_signal(barrier, inc=1, device_id=partner, device_id_type=MESH)
    rim_out[...] = jnp.zeros(rim_out.shape, jnp.float32)
    rho[...] = source[kinds[0]]
    mask_links(lambda mu: links[kinds[0], mu * 18 : mu * 18 + 18], inner_links)
    solve(rho, update, applied, inner_links)
    pl.semaphore_wait(barrier, len(partners))

    started = []

    def send(src, dst, device):
        place = len(started)
        copy = pltpu.make_async_remote_copy(
            src_ref=src, dst_ref=dst, send_sem=send_sem.at[place], recv_sem=recv_sem.at[place],
            device_id=device, device_id_type=MESH,
        )
        copy.start()
        started.append(copy)
        return copy

    def first_links(kind):
        return lambda mu: links[kind, mu * 18 : mu * 18 + 18]

    def second_links(kind):
        return lambda mu: moved_links[kind, mu * 18 : mu * 18 + 18]

    def cross(number, origin, target, links_by_kind):
        load = spin_rows(update)
        from_links, to_links = links_by_kind(origin), links_by_kind(target)
        copies = []
        for place, mu in enumerate((2, 3)):
            lower_device = (ta, gz_prev) if mu == 2 else (ta_prev, gz)
            upper_device = (ta, gz_next) if mu == 2 else (ta_next, gz)
            ahead = project(load, mu, -1)
            behind = adjoint_times(matrix(from_links(mu)), project(load, mu, 1))
            for way, half, device in ((0, ahead, lower_device), (1, behind, upper_device)):
                if mu == 2:
                    out, into = halo_out.at[number, way], halo_in.at[number, way]
                    out[:6] = flat(half[0])
                    out[6:] = flat(half[1])
                else:
                    out, into = rim_out.at[number, way], rim_in.at[number, way]
                    row = 7 * way
                    for k in range(12):
                        out[k : k + 1] = flat(half[k // 6])[k % 6, row : row + 1]
                copies.append(send(out, into, device))
        return copies, to_links

    def plane(origin, target, links_by_kind):
        return cross_plane(
            nothing(), spin_rows(update), links_by_kind(origin), links_by_kind(target),
            (0, 1), edges(7),
        )

    def finish(number, total, copies, to_links):
        time = iota(0)
        rims = []
        for way in range(2):
            copies[2 + way].wait_recv()
            rows = [
                jnp.broadcast_to(rim_in[number, way, k : k + 1], (8, 128)) for k in range(12)
            ]
            rims.append([jnp.stack(rows[p : p + 6]).reshape((2, 3, 8, 128)) for p in (0, 6)])
        total = expand(total, times(matrix(masked(to_links(3), time == 7)), rims[0]), 3, -1)
        total = expand(total, [jnp.where(time == 0, part, 0.0) for part in rims[1]], 3, 1)
        halos = []
        for way in range(2):
            copies[way].wait_recv()
            value = halo_in[number, way]
            halos.append([value[p : p + 6].reshape((2, 3, 8, 128)) for p in (0, 6)])
        total = expand(total, times(matrix(to_links(2)), halos[0]), 2, -1)
        total = expand(total, halos[1], 2, 1)
        return joined(total)

    pending = cross(0, kinds[0], kinds[1], first_links)
    link_copies = [send(upper.at[k], links_in.at[k], (ta_next, gz)) for k in range(2)]
    psi[0] = update[...]
    res[0] = rho[...]
    total = plane(kinds[0], kinds[1], first_links)
    mask_links(first_links(kinds[1]), inner_links)
    hop = finish(0, total, *pending)
    rho[:12] = source[kinds[1], :12] - hop[0]
    rho[12:] = source[kinds[1], 12:] - hop[1]
    solve(rho, update, applied, inner_links)
    pending = cross(1, kinds[1], kinds[0], first_links)
    time_out[0] = upper_pack(rho[:12], rho[12:], low)
    turned = [send(time_out.at[0], time_in.at[0], (ta_next, gz))]
    psi[1] = update[...]
    res[1] = rho[...]
    total = plane(kinds[1], kinds[0], first_links)
    for k in range(2):
        link_copies[k].wait_recv()
        for mu in range(4):
            own = links[k, mu * 18 : mu * 18 + 18]
            real, imag = forward_join(links_in[k, mu * 9 : mu * 9 + 9], own[:9], own[9:], low)
            moved_links[k, mu * 18 : mu * 18 + 9] = real
            moved_links[k, mu * 18 + 9 : mu * 18 + 18] = imag
    mask_links(second_links(kinds[0]), inner_links)
    hop = finish(1, total, *pending)
    own_real, own_imag = res[0, :12] - hop[0], res[0, 12:] - hop[1]
    time_out[1] = upper_pack(own_real, own_imag, low)
    turned.append(send(time_out.at[1], time_in.at[1], (ta_next, gz)))

    turned[0].wait_recv()
    real, imag = forward_join(time_in[0], own_real, own_imag, low)
    rho[:12] = real
    rho[12:] = imag
    solve(rho, update, applied, inner_links)
    pending = cross(2, kinds[0], kinds[1], second_links)
    returned = []
    for k, value in enumerate((update, rho)):
        back[k] = value[...]
        time_out[2 + k] = lower_pack(value[:12], value[12:], low)
        returned.append(send(time_out.at[2 + k], time_in.at[2 + k], (ta_prev, gz)))
    total = plane(kinds[0], kinds[1], second_links)
    mask_links(second_links(kinds[1]), inner_links)
    turned[1].wait_recv()
    own_real, own_imag = forward_join(time_in[1], res[1, :12], res[1, 12:], low)
    hop = finish(2, total, *pending)
    rho[:12] = own_real - hop[0]
    rho[12:] = own_imag - hop[1]
    solve(rho, update, applied, inner_links)

    time_out[4] = lower_pack(update[:12], update[12:], low)
    returned.append(send(time_out.at[4], time_in.at[4], (ta_prev, gz)))
    load = spin_rows(update)
    ahead = project(load, 2, -1)
    behind = adjoint_times(matrix(second_links(kinds[1])(2)), project(load, 2, 1))
    depth = []
    for way, half, column in ((0, ahead, gz_prev), (1, behind, gz_next)):
        half_real, half_imag = flat(half[0]), flat(half[1])
        last_out[way, 1] = lower_pack(half_real, half_imag, low)
        deep = send(last_out.at[way, 1], last_in.at[way, 1], (ta_prev, column))
        last_out[way, 0] = upper_pack(half_real, half_imag, low)
        depth.append(send(last_out.at[way, 0], last_in.at[way, 0], (ta, column)))
        depth.append(deep)
    time_out[5] = lower_pack(rho[:12], rho[12:], low)
    returned.append(send(time_out.at[5], time_in.at[5], (ta_prev, gz)))

    def restored(k, own):
        returned[k].wait_recv()
        return back_join(time_in[2 + k], own[:12], own[12:], low)

    step0 = restored(0, back[0])
    left0 = restored(1, back[1])
    step1 = restored(2, update[...])

    def to_links(mu):
        return jnp.where(low, first_links(kinds[0])(mu), first_links(kinds[1])(mu))

    def from_links(mu):
        return jnp.where(low, first_links(kinds[1])(mu), first_links(kinds[0])(mu))

    applied[:12] = step1[0]
    applied[12:] = step1[1]
    total = cross_plane(nothing(), spin_rows(applied), from_links, to_links, (0, 1, 3), edges(3))
    for way in range(2):
        for half in range(2):
            depth[way * 2 + half].wait_recv()
    for way in range(2):
        high, deep = last_in[way, 0], last_in[way, 1]
        half = (
            jnp.where(low, high, swap_halves(deep)).reshape((2, 3, 8, 128)),
            jnp.where(low, swap_halves(high), deep).reshape((2, 3, 8, 128)),
        )
        if way == 0:
            total = expand(total, times(matrix(to_links(2)), half), 2, -1)
        else:
            total = expand(total, half, 2, 1)
    hop = joined(total)
    left1 = restored(3, rho[...])
    for part in range(2):
        rows = slice(12 * part, 12 * part + 12)
        a, b = step0[part], step1[part]
        solution_out[kinds[0], rows] = psi[0, rows] + jnp.where(low, a, b)
        solution_out[kinds[1], rows] = psi[1, rows] + jnp.where(low, b, a)
        a, b = left0[part] - hop[part], left1[part]
        residual_out[kinds[0], rows] = jnp.where(low, a, b)
        residual_out[kinds[1], rows] = jnp.where(low, b, a)
    for copy in started:
        copy.wait_send()


def per_device(links, source):
    f32 = jnp.float32
    vmem = pl.BlockSpec(memory_space=pltpu.VMEM)
    hbm = pl.BlockSpec(memory_space=pltpu.HBM)
    packed = jax.ShapeDtypeStruct((2,) + FIELD, f32)
    local_links, local_source, upper = pl.pallas_call(
        pack_kernel,
        out_shape=(
            jax.ShapeDtypeStruct((2, 72, 8, 128), f32), packed,
            jax.ShapeDtypeStruct((2, 36, 8, 128), f32),
        ),
        in_specs=[hbm] * 2,
        out_specs=[vmem] * 3,
        scratch_shapes=[
            pltpu.VMEM(links.shape, f32), pltpu.VMEM(source.shape, f32),
            pltpu.SemaphoreType.DMA((5,)),
        ],
        compiler_params=pltpu.CompilerParams(vmem_limit_bytes=24 * 2**20),
    )(links, source)
    copies = 2 + 12 + 2 + 4 + 4
    half = (12, 8, 128)
    result = pl.pallas_call(
        main_kernel,
        out_shape=(packed, packed),
        in_specs=[vmem] * 3,
        out_specs=[vmem] * 2,
        scratch_shapes=[
            pltpu.VMEM((2, 72, 8, 128), f32),
            pltpu.VMEM((3, 18, 8, 128), f32),
            pltpu.VMEM(FIELD, f32),
            pltpu.VMEM(FIELD, f32),
            pltpu.VMEM(FIELD, f32),
            pltpu.VMEM((2,) + FIELD, f32),
            pltpu.VMEM((2,) + FIELD, f32),
            pltpu.VMEM((2,) + FIELD, f32),
            pltpu.VMEM((2, 36, 8, 128), f32),
            pltpu.VMEM((3, 2) + half, f32),
            pltpu.VMEM((3, 2) + half, f32),
            pltpu.VMEM((3, 2, 16, 128), f32),
            pltpu.VMEM((3, 2, 16, 128), f32),
            pltpu.VMEM((6,) + half, f32),
            pltpu.VMEM((6,) + half, f32),
            pltpu.VMEM((2, 2, 6, 8, 128), f32),
            pltpu.VMEM((2, 2, 6, 8, 128), f32),
            pltpu.SemaphoreType.DMA((copies,)),
            pltpu.SemaphoreType.DMA((copies,)),
        ],
        compiler_params=pltpu.CompilerParams(
            collective_id=0, has_side_effects=True, vmem_limit_bytes=32 * 2**20
        ),
    )(local_links, local_source, upper)
    out = jax.ShapeDtypeStruct(source.shape, f32)
    return pl.pallas_call(
        unpack_kernel,
        out_shape=(out, out),
        in_specs=[vmem] * 2,
        out_specs=[hbm] * 2,
        scratch_shapes=[
            pltpu.VMEM(source.shape, f32), pltpu.VMEM(source.shape, f32),
            pltpu.SemaphoreType.DMA((4,)),
        ],
        compiler_params=pltpu.CompilerParams(vmem_limit_bytes=24 * 2**20),
    )(*result)


def solution(mesh):
    in_specs = (P(None, None, "gz", "ta", None), P(None, "gz", "ta", None))
    out_specs = (P(None, "gz", "ta", None), P(None, "gz", "ta", None))
    return jax.shard_map(
        per_device, mesh=mesh, in_specs=in_specs, out_specs=out_specs, check_vma=False
    )
```

```python
import jax
import jax.numpy as jnp
from jax import lax
from jax.experimental import pallas as pl
from jax.experimental.pallas import tpu as pltpu
from jax.sharding import PartitionSpec as P

LX = 16
LY = 16
NMR = 4
BX = LX // 2
BY = LY // 2
BARE = 4.0 + 0.2
EPSILON = 1e-06
COLUMN = ((3, 2, 1, 0), (3, 2, 1, 0), (2, 3, 0, 1), (2, 3, 0, 1))
GAMMA = ((1j, 1j, -1j, -1j), (-1, 1, 1, -1), (1j, -1j, -1j, 1j), (1, 1, 1, 1))
MESH = pl.DeviceIdType.MESH
FIELD = (24, 8, 128)


def iota(dim):
    return lax.broadcasted_iota(jnp.int32, (8, 128), dim)


def turn(value, shift, axis):
    return pltpu.roll(value, shift % value.shape[axis], axis)


def swap_halves(value):
    flat = value.reshape((-1, 8, 128))
    return turn(flat, 4, 1).reshape(value.shape)


def roll_sites(value, shift, axis):
    flat = value.reshape((-1, 8, 128))
    return turn(flat, shift, axis).reshape(value.shape)


def gather_lanes(value, index):
    return jnp.take_along_axis(value, index, axis=1)


def split_tile(tile):
    lane = iota(1)
    low = lane < 64
    cell = lane % 64 // BX * LX + lane % BX
    first = cell + jnp.where(low, 0, BX)
    second = cell + jnp.where(low, BX, 0)
    a, b = tile[:, :128], tile[:, 128:]
    even = jnp.where(low, gather_lanes(a, first), gather_lanes(b, first))
    odd = jnp.where(low, gather_lanes(a, second), gather_lanes(b, second))
    return even, odd


def pack_kernel(links_ref, source_ref, links_out, source_out, upper_out):
    sub_low = iota(0) < 4
    for k in range(24):
        even, odd = split_tile(source_ref[k, 0])
        source_out[0, k] = even
        source_out[1, k] = odd
    for mu in range(4):
        for k in range(9):
            pair = []
            for part in range(2):
                place = mu * 18 + part * 9 + k
                halves = split_tile(links_ref[mu, part * 9 + k, 0])
                for kind in range(2):
                    links_out[kind, place] = halves[kind]
                pair.append(halves)
            for kind in range(2):
                real, imag = pair[0][kind], pair[1][kind]
                upper_out[kind, mu * 9 + k] = jnp.where(sub_low, turn(real, 4, 0), imag)


def unpack_kernel(solution_ref, residual_ref, solution_far, residual_far, solution_out, residual_out, sems):
    lane = iota(1)
    cell = lane // LX * BX + lane % BX
    left = lane % LX < BX
    stores = []
    for source, target, far in (
        (solution_ref, solution_out, solution_far), (residual_ref, residual_out, residual_far)
    ):
        for k in range(24):
            even, odd = source[0, k], source[1, k]
            target[k, 0, :, :128] = jnp.where(left, gather_lanes(even, cell), gather_lanes(odd, cell))
            target[k, 0, :, 128:] = jnp.where(
                left, gather_lanes(odd, cell + 64), gather_lanes(even, cell + 64)
            )
            if k % 12 == 11:
                rows = pl.ds(k - 11, 12)
                copy = pltpu.make_async_copy(target.at[rows], far.at[rows], sems.at[len(stores)])
                copy.start()
                stores.append(copy)
    for copy in stores:
        copy.wait()


def spin_rows(ref):
    return lambda k: (ref[3 * k : 3 * k + 3], ref[12 + 3 * k : 15 + 3 * k])


def add_phase(real, imag, coef, more_real, more_imag):
    if coef == 1:
        return real + more_real, imag + more_imag
    if coef == -1:
        return real - more_real, imag - more_imag
    if coef == 1j:
        return real - more_imag, imag + more_real
    return real + more_imag, imag - more_real


def project(load, mu, sign):
    rows = [
        add_phase(*load(k), sign * GAMMA[mu][k], *load(COLUMN[mu][k])) for k in range(2)
    ]
    return jnp.stack([row[0] for row in rows]), jnp.stack([row[1] for row in rows])


def matrix(link):
    return link[:9].reshape((3, 3, 8, 128)), link[9:].reshape((3, 3, 8, 128))


def times(link, half):
    (ur, ui), (hr, hi) = link, half
    out_real = out_imag = None
    for b in range(3):
        vr, vi = hr[:, b][:, None], hi[:, b][:, None]
        mr, mi = ur[:, b][None], ui[:, b][None]
        pr, pi = mr * vr - mi * vi, mr * vi + mi * vr
        out_real = pr if out_real is None else out_real + pr
        out_imag = pi if out_imag is None else out_imag + pi
    return out_real, out_imag


def adjoint_times(link, half):
    (ur, ui), (hr, hi) = link, half
    out_real = out_imag = None
    for b in range(3):
        vr, vi = hr[:, b][:, None], hi[:, b][:, None]
        mr, mi = ur[b][None], ui[b][None]
        pr, pi = mr * vr + mi * vi, mr * vi - mi * vr
        out_real = pr if out_real is None else out_real + pr
        out_imag = pi if out_imag is None else out_imag + pi
    return out_real, out_imag


def expand(total, half, mu, sign):
    hr, hi = half
    total_real, total_imag = list(total[0]), list(total[1])
    for k in range(4):
        coef = 1 if k < 2 else sign * GAMMA[mu][k]
        other = k if k < 2 else COLUMN[mu][k]
        total_real[k], total_imag[k] = add_phase(
            total_real[k], total_imag[k], coef, hr[other], hi[other]
        )
    return total_real, total_imag


def moved(half, shift, axis):
    return roll_sites(half[0], shift, axis), roll_sites(half[1], shift, axis)


def masked(link, keep):
    return jnp.where(keep[None], link, 0.0)


INNER = {0: (2, -1, 7), 1: (2, -8, -8), 3: (1, -1, -1)}


def edges(time_edge):
    lane, time = iota(1), iota(0)
    return {
        0: lane % BX == BX - 1,
        1: lane // BX % BY == BY - 1,
        3: time == time_edge,
    }


def mask_links(links_of, inner_links):
    edge = edges(7)
    for place, mu in enumerate((0, 1, 3)):
        inner_links[place] = masked(links_of(mu), jnp.logical_not(edge[mu]))


def joined(total):
    return (
        jnp.stack(total[0]).reshape((12, 8, 128)),
        jnp.stack(total[1]).reshape((12, 8, 128)),
    )


def block_operator(ref, inner_links):
    load = spin_rows(ref)
    total = None
    for place, mu in enumerate((0, 1, 3)):
        axis, shift, _ = INNER[mu]
        ahead = moved(project(load, mu, -1), shift, axis)
        if total is None:
            start = [load(k) for k in range(4)]
            total = ([BARE * row[0] for row in start], [BARE * row[1] for row in start])
        total = expand(total, times(matrix(inner_links[place]), ahead), mu, -1)
        behind = adjoint_times(matrix(inner_links[place]), project(load, mu, 1))
        total = expand(total, moved(behind, -shift, axis), mu, 1)
    return joined(total)


def block_weights(rho, applied):
    time = iota(0)
    low = iota(1) < 64
    entries = 12.0 * 8 * BX * BY
    sums = [jnp.zeros((8, 128), jnp.float32)] * 3
    for k in range(12):
        fr, fi, ar, ai = rho[k], rho[12 + k], applied[k], applied[12 + k]
        sums[0] = sums[0] + (ar * fr + ai * fi)
        sums[1] = sums[1] + (ar * fi - ai * fr)
        sums[2] = sums[2] + (ar * ar + ai * ai)
    rows = [jnp.sum(value, axis=0, keepdims=True) for value in sums]
    table = jnp.where(time == 0, rows[0], jnp.where(time == 1, rows[1], rows[2]))
    below = jnp.sum(jnp.where(low, table, 0.0), axis=1, keepdims=True)
    above = jnp.sum(jnp.where(low, 0.0, table), axis=1, keepdims=True)
    table = jnp.where(low, below, above) / entries
    scale = 1.0 / (table[2:3] + EPSILON)
    wr = jnp.broadcast_to(table[0:1] * scale, (8, 128))
    wi = jnp.broadcast_to(table[1:2] * scale, (8, 128))
    return wr, wi


def scaled(wr, wi, ref, k):
    real, imag = ref[k], ref[12 + k]
    return wr * real - wi * imag, wr * imag + wi * real


def solve(rho, update, applied, inner_links):
    update[...] = jnp.zeros(FIELD, jnp.float32)
    first = block_operator(rho, inner_links)
    applied[:12] = first[0]
    applied[12:] = first[1]

    def advance(wr, wi):
        for k in range(12):
            add_real, add_imag = scaled(wr, wi, rho, k)
            update[k] = update[k] + add_real
            update[12 + k] = update[12 + k] + add_imag
            take_real, take_imag = scaled(wr, wi, applied, k)
            rho[k] = rho[k] - take_real
            rho[12 + k] = rho[12 + k] - take_imag

    def step(_, carry):
        wr, wi = block_weights(rho, applied)
        real, imag = block_operator(applied, inner_links)
        advance(wr, wi)
        applied[:12] = applied[:12] - (wr * real - wi * imag)
        applied[12:] = applied[12:] - (wr * imag + wi * real)
        return carry

    lax.fori_loop(0, NMR - 1, step, 0)
    advance(*block_weights(rho, applied))


def nothing():
    zero = jnp.zeros((3, 8, 128), jnp.float32)
    return [zero] * 4, [zero] * 4


def cross_plane(total, load, source_links, target_links, directions, edge):
    for mu in directions:
        axis, inner, shift = INNER[mu]
        ahead = moved(project(load, mu, -1), shift, axis)
        link = matrix(masked(target_links(mu), edge[mu]))
        total = expand(total, times(link, ahead), mu, -1)
        link = matrix(masked(source_links(mu), edge[mu]))
        behind = adjoint_times(link, project(load, mu, 1))
        total = expand(total, moved(behind, -shift, axis), mu, 1)
    return total


def flat(half):
    return half.reshape((6, 8, 128))


def upper_pack(real, imag, low):
    return jnp.where(low, swap_halves(real), imag)


def lower_pack(real, imag, low):
    return jnp.where(low, real, swap_halves(imag))


def forward_join(packed, own_real, own_imag, low):
    real = jnp.where(low, packed, swap_halves(own_real))
    imag = swap_halves(jnp.where(low, own_imag, packed))
    return real, imag


def back_join(packed, own_real, own_imag, low):
    real = swap_halves(jnp.where(low, packed, own_real))
    imag = jnp.where(low, swap_halves(own_imag), packed)
    return real, imag


def main_kernel(
    links, source, upper, solution_out, residual_out,
    moved_links, inner_links, rho, update, applied, psi, res, back,
    links_in, halo_out, halo_in, rim_out, rim_in, time_out, time_in, last_out, last_in, send_sem, recv_sem,
):
    ta, gz = lax.axis_index("ta"), lax.axis_index("gz")
    n_ta, n_gz = lax.axis_size("ta"), lax.axis_size("gz")
    ta_next, ta_prev = lax.rem(ta + 1, n_ta), lax.rem(ta + n_ta - 1, n_ta)
    gz_next, gz_prev = lax.rem(gz + 1, n_gz), lax.rem(gz + n_gz - 1, n_gz)
    here = lax.rem(ta + gz, 2)
    kinds = (here, 1 - here)
    low = iota(0) < 4

    barrier = pltpu.get_barrier_semaphore()
    partners = [
        (ta_next, gz), (ta_prev, gz), (ta, gz_next), (ta, gz_prev),
        (ta_next, gz_next), (ta_next, gz_prev), (ta_prev, gz_next), (ta_prev, gz_prev),
    ]
    for partner in partners:
        pl.semaphore_signal(barrier, inc=1, device_id=partner, device_id_type=MESH)
    rim_out[...] = jnp.zeros(rim_out.shape, jnp.float32)
    rho[...] = source[kinds[0]]
    mask_links(lambda mu: links[kinds[0], mu * 18 : mu * 18 + 18], inner_links)
    solve(rho, update, applied, inner_links)
    pl.semaphore_wait(barrier, len(partners))

    started = []

    def send(src, dst, device):
        place = len(started)
        copy = pltpu.make_async_remote_copy(
            src_ref=src, dst_ref=dst, send_sem=send_sem.at[place], recv_sem=recv_sem.at[place],
            device_id=device, device_id_type=MESH,
        )
        copy.start()
        started.append(copy)
        return copy

    def first_links(kind):
        return lambda mu: links[kind, mu * 18 : mu * 18 + 18]

    def second_links(kind):
        return lambda mu: moved_links[kind, mu * 18 : mu * 18 + 18]

    def cross(number, origin, target, links_by_kind):
        load = spin_rows(update)
        from_links, to_links = links_by_kind(origin), links_by_kind(target)
        copies = []
        for place, mu in enumerate((2, 3)):
            lower_device = (ta, gz_prev) if mu == 2 else (ta_prev, gz)
            upper_device = (ta, gz_next) if mu == 2 else (ta_next, gz)
            for way, device in ((0, lower_device), (1, upper_device)):
                half = project(load, mu, 2 * way - 1)
                if way == 1:
                    half = adjoint_times(matrix(from_links(mu)), half)
                if mu == 2:
                    out, into = halo_out.at[number, way], halo_in.at[number, way]
                    out[:6] = flat(half[0])
                    out[6:] = flat(half[1])
                else:
                    out, into = rim_out.at[number, way], rim_in.at[number, way]
                    row = 7 * way
                    for k in range(12):
                        out[k : k + 1] = flat(half[k // 6])[k % 6, row : row + 1]
                copies.append(send(out, into, device))
        return copies, to_links

    def plane(origin, target, links_by_kind):
        return cross_plane(
            nothing(), spin_rows(update), links_by_kind(origin), links_by_kind(target),
            (0, 1), edges(7),
        )

    def finish(number, total, copies, to_links):
        time = iota(0)
        rims = []
        for way in range(2):
            copies[2 + way].wait_recv()
            rows = [
                jnp.broadcast_to(rim_in[number, way, k : k + 1], (8, 128)) for k in range(12)
            ]
            rims.append([jnp.stack(rows[p : p + 6]).reshape((2, 3, 8, 128)) for p in (0, 6)])
        total = expand(total, times(matrix(masked(to_links(3), time == 7)), rims[0]), 3, -1)
        total = expand(total, [jnp.where(time == 0, part, 0.0) for part in rims[1]], 3, 1)
        halos = []
        for way in range(2):
            copies[way].wait_recv()
            value = halo_in[number, way]
            halos.append([value[p : p + 6].reshape((2, 3, 8, 128)) for p in (0, 6)])
        total = expand(total, times(matrix(to_links(2)), halos[0]), 2, -1)
        total = expand(total, halos[1], 2, 1)
        return joined(total)

    def shift_links(colour):
        link_copies[colour].wait_recv()
        kind = kinds[colour]
        for mu in range(4):
            real, imag = forward_join(
                links_in[kind, mu * 9 : mu * 9 + 9],
                links[kind, mu * 18 : mu * 18 + 9],
                links[kind, mu * 18 + 9 : mu * 18 + 18],
                low,
            )
            moved_links[kind, mu * 18 : mu * 18 + 9] = real
            moved_links[kind, mu * 18 + 9 : mu * 18 + 18] = imag

    pending = cross(0, kinds[0], kinds[1], first_links)
    link_copies = [send(upper.at[kinds[1]], links_in.at[kinds[1]], (ta_next, gz))]
    psi[0] = update[...]
    res[0] = rho[...]
    total = plane(kinds[0], kinds[1], first_links)
    mask_links(first_links(kinds[1]), inner_links)
    hop = finish(0, total, *pending)
    rho[:12] = source[kinds[1], :12] - hop[0]
    rho[12:] = source[kinds[1], 12:] - hop[1]
    solve(rho, update, applied, inner_links)
    pending = cross(1, kinds[1], kinds[0], first_links)
    time_out[0] = upper_pack(rho[:12], rho[12:], low)
    turned = [send(time_out.at[0], time_in.at[0], (ta_next, gz))]
    link_copies.append(send(upper.at[kinds[0]], links_in.at[kinds[0]], (ta_next, gz)))
    psi[1] = update[...]
    res[1] = rho[...]
    total = plane(kinds[1], kinds[0], first_links)
    shift_links(0)
    mask_links(second_links(kinds[0]), inner_links)
    hop = finish(1, total, *pending)
    own_real, own_imag = res[0, :12] - hop[0], res[0, 12:] - hop[1]
    time_out[1] = upper_pack(own_real, own_imag, low)
    turned.append(send(time_out.at[1], time_in.at[1], (ta_next, gz)))

    turned[0].wait_recv()
    real, imag = forward_join(time_in[0], own_real, own_imag, low)
    rho[:12] = real
    rho[12:] = imag
    solve(rho, update, applied, inner_links)
    pending = cross(2, kinds[0], kinds[1], second_links)
    returned = []
    for k, value in enumerate((update, rho)):
        back[k] = value[...]
        time_out[2 + k] = lower_pack(value[:12], value[12:], low)
        returned.append(send(time_out.at[2 + k], time_in.at[2 + k], (ta_prev, gz)))
    shift_links(1)
    total = plane(kinds[0], kinds[1], second_links)
    mask_links(second_links(kinds[1]), inner_links)
    turned[1].wait_recv()
    own_real, own_imag = forward_join(time_in[1], res[1, :12], res[1, 12:], low)
    hop = finish(2, total, *pending)
    rho[:12] = own_real - hop[0]
    rho[12:] = own_imag - hop[1]
    solve(rho, update, applied, inner_links)

    time_out[4] = lower_pack(update[:12], update[12:], low)
    returned.append(send(time_out.at[4], time_in.at[4], (ta_prev, gz)))
    load = spin_rows(update)
    depth = []
    for way, column in ((0, gz_prev), (1, gz_next)):
        half = project(load, 2, 2 * way - 1)
        if way == 1:
            half = adjoint_times(matrix(second_links(kinds[1])(2)), half)
        half_real, half_imag = flat(half[0]), flat(half[1])
        last_out[way, 1] = lower_pack(half_real, half_imag, low)
        deep = send(last_out.at[way, 1], last_in.at[way, 1], (ta_prev, column))
        last_out[way, 0] = upper_pack(half_real, half_imag, low)
        depth.append(send(last_out.at[way, 0], last_in.at[way, 0], (ta, column)))
        depth.append(deep)
    time_out[5] = lower_pack(rho[:12], rho[12:], low)
    returned.append(send(time_out.at[5], time_in.at[5], (ta_prev, gz)))

    def restored(k, own):
        returned[k].wait_recv()
        return back_join(time_in[2 + k], own[:12], own[12:], low)

    step0 = restored(0, back[0])
    left0 = restored(1, back[1])
    step1 = restored(2, update[...])

    def to_links(mu):
        return jnp.where(low, first_links(kinds[0])(mu), first_links(kinds[1])(mu))

    def from_links(mu):
        return jnp.where(low, first_links(kinds[1])(mu), first_links(kinds[0])(mu))

    applied[:12] = step1[0]
    applied[12:] = step1[1]
    total = cross_plane(nothing(), spin_rows(applied), from_links, to_links, (0, 1, 3), edges(3))
    for way in range(2):
        for half in range(2):
            depth[way * 2 + half].wait_recv()
    for way in range(2):
        high, deep = last_in[way, 0], last_in[way, 1]
        half = (
            jnp.where(low, high, swap_halves(deep)).reshape((2, 3, 8, 128)),
            jnp.where(low, swap_halves(high), deep).reshape((2, 3, 8, 128)),
        )
        if way == 0:
            total = expand(total, times(matrix(to_links(2)), half), 2, -1)
        else:
            total = expand(total, half, 2, 1)
    hop = joined(total)
    left1 = restored(3, rho[...])
    for part in range(2):
        rows = slice(12 * part, 12 * part + 12)
        a, b = step0[part], step1[part]
        solution_out[kinds[0], rows] = psi[0, rows] + jnp.where(low, a, b)
        solution_out[kinds[1], rows] = psi[1, rows] + jnp.where(low, b, a)
        a, b = left0[part] - hop[part], left1[part]
        residual_out[kinds[0], rows] = jnp.where(low, a, b)
        residual_out[kinds[1], rows] = jnp.where(low, b, a)
    for copy in started:
        copy.wait_send()


def per_device(links, source):
    f32 = jnp.float32
    vmem = pl.BlockSpec(memory_space=pltpu.VMEM)
    hbm = pl.BlockSpec(memory_space=pltpu.HBM)
    packed = jax.ShapeDtypeStruct((2,) + FIELD, f32)
    local_links, local_source, upper = pl.pallas_call(
        pack_kernel,
        out_shape=(
            jax.ShapeDtypeStruct((2, 72, 8, 128), f32), packed,
            jax.ShapeDtypeStruct((2, 36, 8, 128), f32),
        ),
        in_specs=[vmem] * 2,
        out_specs=[vmem] * 3,
        compiler_params=pltpu.CompilerParams(vmem_limit_bytes=24 * 2**20),
    )(-0.5 * links, source)
    copies = 2 + 12 + 2 + 4 + 4
    half = (12, 8, 128)
    result = pl.pallas_call(
        main_kernel,
        out_shape=(packed, packed),
        in_specs=[vmem] * 3,
        out_specs=[vmem] * 2,
        scratch_shapes=[
            pltpu.VMEM((2, 72, 8, 128), f32),
            pltpu.VMEM((3, 18, 8, 128), f32),
            pltpu.VMEM(FIELD, f32),
            pltpu.VMEM(FIELD, f32),
            pltpu.VMEM(FIELD, f32),
            pltpu.VMEM((2,) + FIELD, f32),
            pltpu.VMEM((2,) + FIELD, f32),
            pltpu.VMEM((2,) + FIELD, f32),
            pltpu.VMEM((2, 36, 8, 128), f32),
            pltpu.VMEM((3, 2) + half, f32),
            pltpu.VMEM((3, 2) + half, f32),
            pltpu.VMEM((3, 2, 16, 128), f32),
            pltpu.VMEM((3, 2, 16, 128), f32),
            pltpu.VMEM((6,) + half, f32),
            pltpu.VMEM((6,) + half, f32),
            pltpu.VMEM((2, 2, 6, 8, 128), f32),
            pltpu.VMEM((2, 2, 6, 8, 128), f32),
            pltpu.SemaphoreType.DMA((copies,)),
            pltpu.SemaphoreType.DMA((copies,)),
        ],
        compiler_params=pltpu.CompilerParams(
            collective_id=0, has_side_effects=True, vmem_limit_bytes=32 * 2**20
        ),
    )(local_links, local_source, upper)
    out = jax.ShapeDtypeStruct(source.shape, f32)
    return pl.pallas_call(
        unpack_kernel,
        out_shape=(out, out),
        in_specs=[vmem] * 2,
        out_specs=[hbm] * 2,
        scratch_shapes=[
            pltpu.VMEM(source.shape, f32), pltpu.VMEM(source.shape, f32),
            pltpu.SemaphoreType.DMA((4,)),
        ],
        compiler_params=pltpu.CompilerParams(vmem_limit_bytes=24 * 2**20),
    )(*result)


def solution(mesh):
    in_specs = (P(None, None, "gz", "ta", None), P(None, "gz", "ta", None))
    out_specs = (P(None, "gz", "ta", None), P(None, "gz", "ta", None))
    return jax.shard_map(
        per_device, mesh=mesh, in_specs=in_specs, out_specs=out_specs, check_vma=False
    )
```

```python
import jax
import jax.numpy as jnp
from jax import lax
from jax.experimental import pallas as pl
from jax.experimental.pallas import tpu as pltpu
from jax.sharding import PartitionSpec as P

LX = 16
LY = 16
NMR = 4
BX = LX // 2
BY = LY // 2
BARE = 4.0 + 0.2
EPSILON = 1e-06
COLUMN = ((3, 2, 1, 0), (3, 2, 1, 0), (2, 3, 0, 1), (2, 3, 0, 1))
GAMMA = ((1j, 1j, -1j, -1j), (-1, 1, 1, -1), (1j, -1j, -1j, 1j), (1, 1, 1, 1))
MESH = pl.DeviceIdType.MESH
FIELD = (24, 8, 128)


def iota(dim):
    return lax.broadcasted_iota(jnp.int32, (8, 128), dim)


def turn(value, shift, axis):
    return pltpu.roll(value, shift % value.shape[axis], axis)


def swap_halves(value):
    flat = value.reshape((-1, 8, 128))
    return turn(flat, 4, 1).reshape(value.shape)


def roll_sites(value, shift, axis):
    flat = value.reshape((-1, 8, 128))
    return turn(flat, shift, axis).reshape(value.shape)


def gather_lanes(value, index):
    return jnp.take_along_axis(value, index, axis=1)


def split_tile(tile):
    lane = iota(1)
    low = lane < 64
    cell = lane % 64 // BX * LX + lane % BX
    first = cell + jnp.where(low, 0, BX)
    second = cell + jnp.where(low, BX, 0)
    a, b = tile[:, :128], tile[:, 128:]
    even = jnp.where(low, gather_lanes(a, first), gather_lanes(b, first))
    odd = jnp.where(low, gather_lanes(a, second), gather_lanes(b, second))
    return even, odd


def pack_kernel(links_ref, source_ref, links_out, source_out, upper_out):
    sub_low = iota(0) < 4
    for k in range(24):
        even, odd = split_tile(source_ref[k, 0])
        source_out[0, k] = even
        source_out[1, k] = odd
    for mu in range(4):
        for k in range(9):
            pair = []
            for part in range(2):
                place = mu * 18 + part * 9 + k
                halves = split_tile(links_ref[mu, part * 9 + k, 0])
                for kind in range(2):
                    links_out[kind, place] = halves[kind]
                pair.append(halves)
            for kind in range(2):
                real, imag = pair[0][kind], pair[1][kind]
                upper_out[kind, mu * 9 + k] = jnp.where(sub_low, turn(real, 4, 0), imag)


def unpack_kernel(solution_ref, residual_ref, solution_far, residual_far, solution_out, residual_out, sems):
    lane = iota(1)
    cell = lane // LX * BX + lane % BX
    left = lane % LX < BX
    stores = []
    for source, target, far in (
        (solution_ref, solution_out, solution_far), (residual_ref, residual_out, residual_far)
    ):
        for k in range(24):
            even, odd = source[0, k], source[1, k]
            target[k, 0, :, :128] = jnp.where(left, gather_lanes(even, cell), gather_lanes(odd, cell))
            target[k, 0, :, 128:] = jnp.where(
                left, gather_lanes(odd, cell + 64), gather_lanes(even, cell + 64)
            )
            if k % 12 == 11:
                rows = pl.ds(k - 11, 12)
                copy = pltpu.make_async_copy(target.at[rows], far.at[rows], sems.at[len(stores)])
                copy.start()
                stores.append(copy)
    for copy in stores:
        copy.wait()


def spin_rows(ref):
    return lambda k: (ref[3 * k : 3 * k + 3], ref[12 + 3 * k : 15 + 3 * k])


def add_phase(real, imag, coef, more_real, more_imag):
    if coef == 1:
        return real + more_real, imag + more_imag
    if coef == -1:
        return real - more_real, imag - more_imag
    if coef == 1j:
        return real - more_imag, imag + more_real
    return real + more_imag, imag - more_real


def project(load, mu, sign):
    rows = [
        add_phase(*load(k), sign * GAMMA[mu][k], *load(COLUMN[mu][k])) for k in range(2)
    ]
    return jnp.stack([row[0] for row in rows]), jnp.stack([row[1] for row in rows])


def matrix(link):
    return link[:9].reshape((3, 3, 8, 128)), link[9:].reshape((3, 3, 8, 128))


def times(link, half):
    (ur, ui), (hr, hi) = link, half
    out_real = out_imag = None
    for b in range(3):
        vr, vi = hr[:, b][:, None], hi[:, b][:, None]
        mr, mi = ur[:, b][None], ui[:, b][None]
        pr, pi = mr * vr - mi * vi, mr * vi + mi * vr
        out_real = pr if out_real is None else out_real + pr
        out_imag = pi if out_imag is None else out_imag + pi
    return out_real, out_imag


def adjoint_times(link, half):
    (ur, ui), (hr, hi) = link, half
    out_real = out_imag = None
    for b in range(3):
        vr, vi = hr[:, b][:, None], hi[:, b][:, None]
        mr, mi = ur[b][None], ui[b][None]
        pr, pi = mr * vr + mi * vi, mr * vi - mi * vr
        out_real = pr if out_real is None else out_real + pr
        out_imag = pi if out_imag is None else out_imag + pi
    return out_real, out_imag


def expand(total, half, mu, sign):
    hr, hi = half
    total_real, total_imag = list(total[0]), list(total[1])
    for k in range(4):
        coef = 1 if k < 2 else sign * GAMMA[mu][k]
        other = k if k < 2 else COLUMN[mu][k]
        total_real[k], total_imag[k] = add_phase(
            total_real[k], total_imag[k], coef, hr[other], hi[other]
        )
    return total_real, total_imag


def moved(half, shift, axis):
    return roll_sites(half[0], shift, axis), roll_sites(half[1], shift, axis)


def masked(link, keep):
    return jnp.where(keep[None], link, 0.0)


INNER = {0: (2, -1, 7), 1: (2, -8, -8), 3: (1, -1, -1)}


def edges(time_edge):
    lane, time = iota(1), iota(0)
    return {
        0: lane % BX == BX - 1,
        1: lane // BX % BY == BY - 1,
        3: time == time_edge,
    }


def mask_links(links_of, inner_links):
    edge = edges(7)
    for place, mu in enumerate((0, 1, 3)):
        inner_links[place] = masked(links_of(mu), jnp.logical_not(edge[mu]))


def joined(total):
    return (
        jnp.stack(total[0]).reshape((12, 8, 128)),
        jnp.stack(total[1]).reshape((12, 8, 128)),
    )


def block_operator(ref, inner_links):
    load = spin_rows(ref)
    total = None
    for place, mu in enumerate((0, 1, 3)):
        axis, shift, _ = INNER[mu]
        ahead = moved(project(load, mu, -1), shift, axis)
        if total is None:
            start = [load(k) for k in range(4)]
            total = ([BARE * row[0] for row in start], [BARE * row[1] for row in start])
        total = expand(total, times(matrix(inner_links[place]), ahead), mu, -1)
        behind = adjoint_times(matrix(inner_links[place]), project(load, mu, 1))
        total = expand(total, moved(behind, -shift, axis), mu, 1)
    return joined(total)


def block_weights(rho, applied):
    time = iota(0)
    low = iota(1) < 64
    entries = 12.0 * 8 * BX * BY
    sums = [jnp.zeros((8, 128), jnp.float32)] * 3
    for k in range(12):
        fr, fi, ar, ai = rho[k], rho[12 + k], applied[k], applied[12 + k]
        sums[0] = sums[0] + (ar * fr + ai * fi)
        sums[1] = sums[1] + (ar * fi - ai * fr)
        sums[2] = sums[2] + (ar * ar + ai * ai)
    rows = [jnp.sum(value, axis=0, keepdims=True) for value in sums]
    table = jnp.where(time == 0, rows[0], jnp.where(time == 1, rows[1], rows[2]))
    below = jnp.sum(jnp.where(low, table, 0.0), axis=1, keepdims=True)
    above = jnp.sum(jnp.where(low, 0.0, table), axis=1, keepdims=True)
    table = jnp.where(low, below, above) / entries
    scale = 1.0 / (table[2:3] + EPSILON)
    wr = jnp.broadcast_to(table[0:1] * scale, (8, 128))
    wi = jnp.broadcast_to(table[1:2] * scale, (8, 128))
    return wr, wi


def scaled(wr, wi, ref, k):
    real, imag = ref[k], ref[12 + k]
    return wr * real - wi * imag, wr * imag + wi * real


def settle(rho, applied, wr, wi):
    for k in range(12):
        take_real, take_imag = scaled(wr, wi, applied, k)
        rho[k] = rho[k] - take_real
        rho[12 + k] = rho[12 + k] - take_imag


def solve(rho, update, applied, inner_links):
    update[...] = jnp.zeros(FIELD, jnp.float32)
    first = block_operator(rho, inner_links)
    applied[:12] = first[0]
    applied[12:] = first[1]

    def advance(wr, wi):
        for k in range(12):
            add_real, add_imag = scaled(wr, wi, rho, k)
            update[k] = update[k] + add_real
            update[12 + k] = update[12 + k] + add_imag

    def step(_, carry):
        wr, wi = block_weights(rho, applied)
        real, imag = block_operator(applied, inner_links)
        advance(wr, wi)
        settle(rho, applied, wr, wi)
        applied[:12] = applied[:12] - (wr * real - wi * imag)
        applied[12:] = applied[12:] - (wr * imag + wi * real)
        return carry

    lax.fori_loop(0, NMR - 1, step, 0)
    weights = block_weights(rho, applied)
    advance(*weights)
    return weights


def nothing():
    zero = jnp.zeros((3, 8, 128), jnp.float32)
    return [zero] * 4, [zero] * 4


def cross_plane(total, load, source_links, target_links, directions, edge):
    for mu in directions:
        axis, inner, shift = INNER[mu]
        ahead = moved(project(load, mu, -1), shift, axis)
        link = matrix(masked(target_links(mu), edge[mu]))
        total = expand(total, times(link, ahead), mu, -1)
        link = matrix(masked(source_links(mu), edge[mu]))
        behind = adjoint_times(link, project(load, mu, 1))
        total = expand(total, moved(behind, -shift, axis), mu, 1)
    return total


def flat(half):
    return half.reshape((6, 8, 128))


def upper_pack(real, imag, low):
    return jnp.where(low, swap_halves(real), imag)


def lower_pack(real, imag, low):
    return jnp.where(low, real, swap_halves(imag))


def forward_join(packed, own_real, own_imag, low):
    real = jnp.where(low, packed, swap_halves(own_real))
    imag = swap_halves(jnp.where(low, own_imag, packed))
    return real, imag


def back_join(packed, own_real, own_imag, low):
    real = swap_halves(jnp.where(low, packed, own_real))
    imag = jnp.where(low, swap_halves(own_imag), packed)
    return real, imag


def main_kernel(
    links, source, upper, solution_out, residual_out,
    moved_links, inner_links, rho, update, applied, psi, res, back,
    links_in, halo_out, halo_in, rim_out, rim_in, time_out, time_in, last_out, last_in, send_sem, recv_sem,
):
    ta, gz = lax.axis_index("ta"), lax.axis_index("gz")
    n_ta, n_gz = lax.axis_size("ta"), lax.axis_size("gz")
    ta_next, ta_prev = lax.rem(ta + 1, n_ta), lax.rem(ta + n_ta - 1, n_ta)
    gz_next, gz_prev = lax.rem(gz + 1, n_gz), lax.rem(gz + n_gz - 1, n_gz)
    here = lax.rem(ta + gz, 2)
    kinds = (here, 1 - here)
    low = iota(0) < 4

    barrier = pltpu.get_barrier_semaphore()
    partners = [
        (ta_next, gz), (ta_prev, gz), (ta, gz_next), (ta, gz_prev),
        (ta_next, gz_next), (ta_next, gz_prev), (ta_prev, gz_next), (ta_prev, gz_prev),
    ]
    for partner in partners:
        pl.semaphore_signal(barrier, inc=1, device_id=partner, device_id_type=MESH)
    rim_out[...] = jnp.zeros(rim_out.shape, jnp.float32)
    rho[...] = source[kinds[0]]
    mask_links(lambda mu: links[kinds[0], mu * 18 : mu * 18 + 18], inner_links)
    weights = solve(rho, update, applied, inner_links)
    pl.semaphore_wait(barrier, len(partners))

    started = []

    def send(src, dst, device):
        place = len(started)
        copy = pltpu.make_async_remote_copy(
            src_ref=src, dst_ref=dst, send_sem=send_sem.at[place], recv_sem=recv_sem.at[place],
            device_id=device, device_id_type=MESH,
        )
        copy.start()
        started.append(copy)
        return copy

    def first_links(kind):
        return lambda mu: links[kind, mu * 18 : mu * 18 + 18]

    def second_links(kind):
        return lambda mu: moved_links[kind, mu * 18 : mu * 18 + 18]

    def cross(number, origin, target, links_by_kind):
        load = spin_rows(update)
        from_links, to_links = links_by_kind(origin), links_by_kind(target)
        copies = []
        for place, mu in enumerate((2, 3)):
            lower_device = (ta, gz_prev) if mu == 2 else (ta_prev, gz)
            upper_device = (ta, gz_next) if mu == 2 else (ta_next, gz)
            for way, device in ((0, lower_device), (1, upper_device)):
                half = project(load, mu, 2 * way - 1)
                if way == 1:
                    half = adjoint_times(matrix(from_links(mu)), half)
                if mu == 2:
                    out, into = halo_out.at[number, way], halo_in.at[number, way]
                    out[:6] = flat(half[0])
                    out[6:] = flat(half[1])
                else:
                    out, into = rim_out.at[number, way], rim_in.at[number, way]
                    row = 7 * way
                    for k in range(12):
                        out[k : k + 1] = flat(half[k // 6])[k % 6, row : row + 1]
                copies.append(send(out, into, device))
        return copies, to_links

    def plane(origin, target, links_by_kind):
        return cross_plane(
            nothing(), spin_rows(update), links_by_kind(origin), links_by_kind(target),
            (0, 1), edges(7),
        )

    def finish(number, total, copies, to_links):
        time = iota(0)
        rims = []
        for way in range(2):
            copies[2 + way].wait_recv()
            rows = [
                jnp.broadcast_to(rim_in[number, way, k : k + 1], (8, 128)) for k in range(12)
            ]
            rims.append([jnp.stack(rows[p : p + 6]).reshape((2, 3, 8, 128)) for p in (0, 6)])
        total = expand(total, times(matrix(masked(to_links(3), time == 7)), rims[0]), 3, -1)
        total = expand(total, [jnp.where(time == 0, part, 0.0) for part in rims[1]], 3, 1)
        halos = []
        for way in range(2):
            copies[way].wait_recv()
            value = halo_in[number, way]
            halos.append([value[p : p + 6].reshape((2, 3, 8, 128)) for p in (0, 6)])
        total = expand(total, times(matrix(to_links(2)), halos[0]), 2, -1)
        total = expand(total, halos[1], 2, 1)
        return joined(total)

    def shift_links(colour):
        link_copies[colour].wait_recv()
        kind = kinds[colour]
        for mu in range(4):
            real, imag = forward_join(
                links_in[kind, mu * 9 : mu * 9 + 9],
                links[kind, mu * 18 : mu * 18 + 9],
                links[kind, mu * 18 + 9 : mu * 18 + 18],
                low,
            )
            moved_links[kind, mu * 18 : mu * 18 + 9] = real
            moved_links[kind, mu * 18 + 9 : mu * 18 + 18] = imag

    pending = cross(0, kinds[0], kinds[1], first_links)
    link_copies = [send(upper.at[kinds[1]], links_in.at[kinds[1]], (ta_next, gz))]
    settle(rho, applied, *weights)
    psi[0] = update[...]
    res[0] = rho[...]
    total = plane(kinds[0], kinds[1], first_links)
    mask_links(first_links(kinds[1]), inner_links)
    hop = finish(0, total, *pending)
    rho[:12] = source[kinds[1], :12] - hop[0]
    rho[12:] = source[kinds[1], 12:] - hop[1]
    weights = solve(rho, update, applied, inner_links)
    pending = cross(1, kinds[1], kinds[0], first_links)
    settle(rho, applied, *weights)
    time_out[0] = upper_pack(rho[:12], rho[12:], low)
    turned = [send(time_out.at[0], time_in.at[0], (ta_next, gz))]
    link_copies.append(send(upper.at[kinds[0]], links_in.at[kinds[0]], (ta_next, gz)))
    psi[1] = update[...]
    res[1] = rho[...]
    total = plane(kinds[1], kinds[0], first_links)
    shift_links(0)
    mask_links(second_links(kinds[0]), inner_links)
    hop = finish(1, total, *pending)
    own_real, own_imag = res[0, :12] - hop[0], res[0, 12:] - hop[1]
    time_out[1] = upper_pack(own_real, own_imag, low)
    turned.append(send(time_out.at[1], time_in.at[1], (ta_next, gz)))

    turned[0].wait_recv()
    real, imag = forward_join(time_in[0], own_real, own_imag, low)
    rho[:12] = real
    rho[12:] = imag
    weights = solve(rho, update, applied, inner_links)
    pending = cross(2, kinds[0], kinds[1], second_links)
    settle(rho, applied, *weights)
    returned = []
    for k, value in enumerate((update, rho)):
        back[k] = value[...]
        time_out[2 + k] = lower_pack(value[:12], value[12:], low)
        returned.append(send(time_out.at[2 + k], time_in.at[2 + k], (ta_prev, gz)))
    shift_links(1)
    total = plane(kinds[0], kinds[1], second_links)
    mask_links(second_links(kinds[1]), inner_links)
    turned[1].wait_recv()
    own_real, own_imag = forward_join(time_in[1], res[1, :12], res[1, 12:], low)
    hop = finish(2, total, *pending)
    rho[:12] = own_real - hop[0]
    rho[12:] = own_imag - hop[1]
    weights = solve(rho, update, applied, inner_links)

    time_out[4] = lower_pack(update[:12], update[12:], low)
    returned.append(send(time_out.at[4], time_in.at[4], (ta_prev, gz)))
    load = spin_rows(update)
    depth = []
    for way, column in ((0, gz_prev), (1, gz_next)):
        half = project(load, 2, 2 * way - 1)
        if way == 1:
            half = adjoint_times(matrix(second_links(kinds[1])(2)), half)
        half_real, half_imag = flat(half[0]), flat(half[1])
        last_out[way, 1] = lower_pack(half_real, half_imag, low)
        deep = send(last_out.at[way, 1], last_in.at[way, 1], (ta_prev, column))
        last_out[way, 0] = upper_pack(half_real, half_imag, low)
        depth.append(send(last_out.at[way, 0], last_in.at[way, 0], (ta, column)))
        depth.append(deep)
    settle(rho, applied, *weights)
    time_out[5] = lower_pack(rho[:12], rho[12:], low)
    returned.append(send(time_out.at[5], time_in.at[5], (ta_prev, gz)))

    def restored(k, own):
        returned[k].wait_recv()
        return back_join(time_in[2 + k], own[:12], own[12:], low)

    step0 = restored(0, back[0])
    left0 = restored(1, back[1])
    step1 = restored(2, update[...])

    def to_links(mu):
        return jnp.where(low, first_links(kinds[0])(mu), first_links(kinds[1])(mu))

    def from_links(mu):
        return jnp.where(low, first_links(kinds[1])(mu), first_links(kinds[0])(mu))

    applied[:12] = step1[0]
    applied[12:] = step1[1]
    total = cross_plane(nothing(), spin_rows(applied), from_links, to_links, (0, 1, 3), edges(3))
    for way in range(2):
        for half in range(2):
            depth[way * 2 + half].wait_recv()
    for way in range(2):
        high, deep = last_in[way, 0], last_in[way, 1]
        half = (
            jnp.where(low, high, swap_halves(deep)).reshape((2, 3, 8, 128)),
            jnp.where(low, swap_halves(high), deep).reshape((2, 3, 8, 128)),
        )
        if way == 0:
            total = expand(total, times(matrix(to_links(2)), half), 2, -1)
        else:
            total = expand(total, half, 2, 1)
    hop = joined(total)
    left1 = restored(3, rho[...])
    for part in range(2):
        rows = slice(12 * part, 12 * part + 12)
        a, b = step0[part], step1[part]
        solution_out[kinds[0], rows] = psi[0, rows] + jnp.where(low, a, b)
        solution_out[kinds[1], rows] = psi[1, rows] + jnp.where(low, b, a)
        a, b = left0[part] - hop[part], left1[part]
        residual_out[kinds[0], rows] = jnp.where(low, a, b)
        residual_out[kinds[1], rows] = jnp.where(low, b, a)
    for copy in started:
        copy.wait_send()


def per_device(links, source):
    f32 = jnp.float32
    vmem = pl.BlockSpec(memory_space=pltpu.VMEM)
    hbm = pl.BlockSpec(memory_space=pltpu.HBM)
    packed = jax.ShapeDtypeStruct((2,) + FIELD, f32)
    local_links, local_source, upper = pl.pallas_call(
        pack_kernel,
        out_shape=(
            jax.ShapeDtypeStruct((2, 72, 8, 128), f32), packed,
            jax.ShapeDtypeStruct((2, 36, 8, 128), f32),
        ),
        in_specs=[vmem] * 2,
        out_specs=[vmem] * 3,
        compiler_params=pltpu.CompilerParams(vmem_limit_bytes=24 * 2**20),
    )(-0.5 * links, source)
    copies = 2 + 12 + 2 + 4 + 4
    half = (12, 8, 128)
    result = pl.pallas_call(
        main_kernel,
        out_shape=(packed, packed),
        in_specs=[vmem] * 3,
        out_specs=[vmem] * 2,
        scratch_shapes=[
            pltpu.VMEM((2, 72, 8, 128), f32),
            pltpu.VMEM((3, 18, 8, 128), f32),
            pltpu.VMEM(FIELD, f32),
            pltpu.VMEM(FIELD, f32),
            pltpu.VMEM(FIELD, f32),
            pltpu.VMEM((2,) + FIELD, f32),
            pltpu.VMEM((2,) + FIELD, f32),
            pltpu.VMEM((2,) + FIELD, f32),
            pltpu.VMEM((2, 36, 8, 128), f32),
            pltpu.VMEM((3, 2) + half, f32),
            pltpu.VMEM((3, 2) + half, f32),
            pltpu.VMEM((3, 2, 16, 128), f32),
            pltpu.VMEM((3, 2, 16, 128), f32),
            pltpu.VMEM((6,) + half, f32),
            pltpu.VMEM((6,) + half, f32),
            pltpu.VMEM((2, 2, 6, 8, 128), f32),
            pltpu.VMEM((2, 2, 6, 8, 128), f32),
            pltpu.SemaphoreType.DMA((copies,)),
            pltpu.SemaphoreType.DMA((copies,)),
        ],
        compiler_params=pltpu.CompilerParams(
            collective_id=0, has_side_effects=True, vmem_limit_bytes=32 * 2**20
        ),
    )(local_links, local_source, upper)
    out = jax.ShapeDtypeStruct(source.shape, f32)
    return pl.pallas_call(
        unpack_kernel,
        out_shape=(out, out),
        in_specs=[vmem] * 2,
        out_specs=[hbm] * 2,
        scratch_shapes=[
            pltpu.VMEM(source.shape, f32), pltpu.VMEM(source.shape, f32),
            pltpu.SemaphoreType.DMA((4,)),
        ],
        compiler_params=pltpu.CompilerParams(vmem_limit_bytes=24 * 2**20),
    )(*result)


def solution(mesh):
    in_specs = (P(None, None, "gz", "ta", None), P(None, "gz", "ta", None))
    out_specs = (P(None, "gz", "ta", None), P(None, "gz", "ta", None))
    return jax.shard_map(
        per_device, mesh=mesh, in_specs=in_specs, out_specs=out_specs, check_vma=False
    )
```
